128 devices in a mesh: passage: 2 (over x_hi), brick: 64 (over z, y, x_lo, core).
Axes of the slice: x: 4 (x_hi: 2, x_lo: 2; x = x_hi * 2 + x_lo), y: 4, z: 4, core: 2. Of those that a mesh axis runs over, the one named last changes fastest.
Arguments:
- jac_blocks: bfloat16 [2, 25, 64, 8192], P('passage', None, None, 'brick'), may hold values from -6 to 6
- psi_start: float32 [2, 10, 64, 64, 128], P('passage', None, 'brick'), may hold values from -6 to 6
- source: float32 [2, 10, 64, 64, 128], P('passage', None, 'brick'), may hold values from -6 to 6
- pseudo_step: float32 [2, 64, 64, 128], P('passage', 'brick'), may hold values from 0.1 to 0.4
- dissipation: float32 [2, 64, 64, 128], P('passage', 'brick'), may hold values from 0.04 to 0.15
- freq_volume: float32 [2, 64, 64, 128], P('passage', 'brick'), may hold values from 0.2 to 2
- normals: float32 [2, 3, 64, 64], P('passage', None, 'brick'), may hold values from -6 to 6
- face_owner: int32 [2, 4096, 1], P('passage', 'brick'), may hold values from 0 to 63; in each aligned block of 64 rows (0 to 63, 64 to 127, ..., all dimensions but the last counted through in order) at most 4 rows name the same one
- face_slot: int32 [2, 4096], P('passage', 'brick'), may hold values from 0 to 255
Outputs:
- adjoint: float32 [2, 10, 64, 64, 128], P('passage', None, 'brick')
- sensitivity: float32 [2, 6, 16384], P('passage', None, 'brick')
The draws below stay inside these ranges and needn't reach their ends.
Inputs may be any that keep to these rules, and one draw needn't show every extreme that they name: `face_owner`: in the 64 faces of one device (aligned blocks of the rows), no brick is named by more than 4 faces, and in some block some brick is named by exactly 4.
All inputs are finite; a program needn't handle non-finite values.
Results may differ from the reference program's by a relative error of at most 0.0003.
Values may be sent and summed in bfloat16 or wider, within the bound.
No kernel may reach another device: no remote copies, remote signals or barrier semaphores. Data moves between devices by JAX's collectives and lax.ppermute only.
A program may use at most 64 MiB of HBM per device.

```python
import math
import jax
import jax.numpy as jnp
import numpy as np

PASSAGES = 2
CI = 1
NJ = 64
NK = 128
NI = 64
NJK = 8192
NODE_DEV = 256
NODES = 16384
CAP = 4
SWEEPS = 2
ND = 1
BLADES = 36
N_BRICK = 64


def plant(array, stream_key, least, largest):
    dims = array.shape
    spot = [jax.random.randint(jax.random.fold_in(stream_key, axis), (), 0, dims[axis]) for axis in range(len(dims))]
    array = array.at[tuple(spot)].set(least)
    longest = dims.index(max(dims))
    spot[longest] = (spot[longest] + 1) % dims[longest]
    return array.at[tuple(spot)].set(largest)


def block_levels(own_key, extent, shards, smallest, largest):
    def one(axis_at, blocks):
        steps = jax.random.uniform(jax.random.fold_in(jax.random.fold_in(own_key, 6), axis_at), (blocks,), jnp.float32, smallest / len(shards), largest / len(shards))
        return jnp.repeat(jnp.exp(steps), extent[axis_at] // blocks).reshape((-1,) + (1,) * (len(extent) - axis_at - 1))

    level = one(*shards[0])
    for cut in shards[1:]:
        level = level * one(*cut)
    return level


def routed_block(key, own, number, rows, number_of, top, most, slope):
    sequence = jax.random.permutation(key, number_of)
    crowded, ordinary = shares(number_of, rows * top, most, slope, True), shares(number_of, rows * top, most, slope, False)
    places = jnp.arange(number_of)

    def named(sizes, turn):
        used = int((sizes > 0).sum())
        fixed = max(1, used // 4)
        shifted = fixed + (places - fixed + turn * (used - fixed)) % max(1, number_of - fixed)
        return jnp.zeros((number_of,), jnp.int32).at[sequence[jnp.where(places < fixed, places, shifted)]].set(jnp.asarray(sizes, jnp.int32))

    sizes = jnp.where(number % 4 == 0, named(crowded, number // 4), named(ordinary, number - number // 4 - 1))
    mixed = jax.random.permutation(jax.random.fold_in(own, 3), number_of)
    donor, sink = mixed[0:number_of // 2 * 2:2], mixed[1:number_of // 2 * 2:2]
    slack = jnp.minimum(sizes[donor] - 1, most - sizes[sink]) // 2
    slack = jnp.where((donor == sequence[0]) | (sink == sequence[0]) | (sizes[sink] == 0), 0, jnp.maximum(slack, 0))
    shifted = jax.random.randint(jax.random.fold_in(own, 4), (number_of // 2,), 0, 1 << 20) % (slack + 1)
    sizes = sizes.at[donor].add(-shifted).at[sink].add(shifted)
    members = jnp.searchsorted(jnp.cumsum(sizes), jnp.arange(rows * top), side="right").astype(jnp.int32)
    table = members.reshape(top, rows).T
    table = table[jax.random.permutation(jax.random.fold_in(own, 1), rows)]
    turn = jax.random.randint(jax.random.fold_in(own, 2), (rows, 1), 0, top)
    return jnp.take_along_axis(table, (jnp.arange(top)[None, :] + turn) % top, axis=1)


def shares(count, total, most, skew, full):
    loads = [(1 << 20) // math.isqrt(rank ** skew) + 1 for rank in range(1, count + 1)]
    largest = most if full else min(most, max(-(-total // count), total * loads[0] // sum(loads)))
    least = 1 if total - largest >= count - 1 else 0
    counts, rest = [largest] + [least] * (count - 1), total - largest - least * (count - 1)
    while rest > 0:
        candidates = [i for i in range(1, count) if counts[i] < largest] or [i for i in range(1, count) if counts[i] < most]
        mass, budget = sum([loads[i] for i in candidates]), rest
        for i in candidates:
            more = min(most - counts[i], max(1, budget * loads[i] // mass), rest)
            counts[i] = counts[i] + more
            rest = rest - more
    return np.array(counts)


def noise(key, shape, spread, limit, shards=(), dtype=jnp.bfloat16):
    values = spread * jax.random.normal(key, shape, jnp.float32)
    if shards:
        values = values * block_levels(key, shape, shards, -0.22, 0.18)
    return jnp.clip(values, -limit, limit).astype(dtype)


def setup_inputs(seed: int = 0) -> dict:
    seeds = jax.random.split(jax.random.key(seed), 10)
    jac_blocks = noise(seeds[0], (PASSAGES, 25, NI, NJK), 0.4, 6.0, ((0, 2), (3, 64)))
    psi_start = noise(seeds[1], (PASSAGES, 10, NI, NJ, NK), 1.0, 6.0, ((0, 2), (2, 64)), jnp.float32)
    source = noise(seeds[2], (PASSAGES, 10, NI, NJ, NK), 1.0, 6.0, ((0, 2), (2, 64)), jnp.float32)
    pseudo_step = jnp.clip(jnp.exp(math.log(0.4) - 1.3862944 * jax.random.uniform(seeds[3], (PASSAGES, NI, NJ, NK), jnp.float32) ** block_levels(seeds[3], (PASSAGES, NI, NJ, NK), ((0, 2), (1, 64)), -0.2, 0.2)), 0.1, 0.4)
    dissipation = jnp.clip(jnp.exp(math.log(0.15) - 1.3217559 * jax.random.uniform(seeds[4], (PASSAGES, NI, NJ, NK), jnp.float32) ** block_levels(seeds[4], (PASSAGES, NI, NJ, NK), ((0, 2), (1, 64)), -0.2, 0.2)), 0.04, 0.15)
    freq_volume = jnp.clip(jnp.exp(math.log(2.0) - 2.3025851 * jax.random.uniform(seeds[5], (PASSAGES, NI, NJ, NK), jnp.float32) ** block_levels(seeds[5], (PASSAGES, NI, NJ, NK), ((0, 2), (1, 64)), -0.2, 0.2)), 0.2, 2.0)
    normals = noise(seeds[6], (PASSAGES, 3, NI, NJ), 1.0, 6.0, ((0, 2), (2, 64)), jnp.float32)
    face_owner_keys = jax.random.split(jax.random.fold_in(seeds[7], 1), PASSAGES * (NI * NJ) // (CI * NJ))
    face_owner_turns = jax.random.permutation(jax.random.fold_in(seeds[7], 3), PASSAGES * (NI * NJ) // (CI * NJ))
    face_owner = jax.vmap(lambda own, number: routed_block(jax.random.fold_in(seeds[7], 2), own, number, CI * NJ, N_BRICK, 1, CAP, 2))(face_owner_keys, face_owner_turns).reshape((PASSAGES, NI * NJ, 1))
    face_slot = plant(jax.random.randint(seeds[8], (PASSAGES, NI * NJ), 0, NODE_DEV), jax.random.fold_in(seeds[8], 1), 0, NODE_DEV - 1).astype(jnp.int32)
    return dict(jac_blocks=jac_blocks, psi_start=psi_start, source=source, pseudo_step=pseudo_step, dissipation=dissipation, freq_volume=freq_volume, normals=normals, face_owner=face_owner, face_slot=face_slot)


def rotate(rim, turn):
    cosine = math.cos(turn)
    sine = math.sin(turn)
    real_part = rim[:, :5]
    imag_part = rim[:, 5:]
    return jnp.concatenate([real_part * cosine - imag_part * sine, real_part * sine + imag_part * cosine], axis=1)


def transpose_apply(tiles, diff):
    total_real = jnp.zeros_like(diff[:, :5])
    total_imag = jnp.zeros_like(diff[:, :5])
    for row_index in range(5):
        column = tiles[:, row_index * 5:row_index * 5 + 5].astype(jnp.float32)
        total_real = total_real + column * diff[:, row_index:row_index + 1]
        total_imag = total_imag + column * diff[:, 5 + row_index:6 + row_index]
    return jnp.concatenate([total_real, total_imag], axis=1)


def reference(jac_blocks, psi_start, source, pseudo_step, dissipation, freq_volume, normals, face_owner, face_slot):
    passes = psi_start.shape[0]
    phase_angle = 2.0 * math.pi * ND * passes / BLADES
    tiles = jac_blocks.reshape(passes, 25, NI, NJ, NK)
    cycle_index = jnp.arange(passes).reshape(passes, 1, 1, 1, 1)
    state = psi_start
    for sweep in range(SWEEPS):
        below_rim = jnp.roll(state[:, :, :, -1:], 1, axis=0)
        below_rim = jnp.where(cycle_index == 0, rotate(below_rim, -phase_angle), below_rim)
        above_rim = jnp.roll(state[:, :, :, :1], -1, axis=0)
        above_rim = jnp.where(cycle_index == passes - 1, rotate(above_rim, phase_angle), above_rim)
        padded_j = jnp.concatenate([below_rim, state, above_rim], axis=3)
        padded_i = jnp.pad(state, ((0, 0), (0, 0), (1, 1), (0, 0), (0, 0)))
        padded_k = jnp.pad(state, ((0, 0), (0, 0), (0, 0), (0, 0), (1, 1)))
        beside = padded_i[:, :, 2:] + padded_i[:, :, :-2]
        beside = beside + padded_j[:, :, :, 2:] + padded_j[:, :, :, :-2]
        beside = beside + padded_k[..., 2:] + padded_k[..., :-2]
        diff = 0.5 * (padded_i[:, :, 2:] - padded_i[:, :, :-2])
        convect = transpose_apply(tiles, diff)
        omega = freq_volume[:, None]
        spin = jnp.concatenate([omega * state[:, 5:], -omega * state[:, :5]], axis=1)
        resid = convect + spin + dissipation[:, None] * (6.0 * state - beside) - source
        state = state - pseudo_step[:, None] * resid
    wall_state = state[..., 0]
    values = jnp.concatenate([normals * wall_state[:, 1:4], normals * wall_state[:, 6:9]], axis=1)
    values = values.reshape(passes, 6, NI * NJ)
    node_ids = (face_owner[..., 0] * NODE_DEV + face_slot).astype(jnp.int32)
    results = []
    for part_index in range(passes):
        summed = jnp.zeros((6, NODES), jnp.float32).at[:, node_ids[part_index]].add(values[part_index])
        results.append(summed)
    return state, jnp.stack(results, axis=0)
```

```python
import functools
import math

import jax
import jax.numpy as jnp
from jax import lax
from jax.experimental import pallas as pl
from jax.experimental.pallas import tpu as pltpu
from jax.sharding import PartitionSpec as P

NODE_DEV = 256
CAP = 4
ND = 1
BLADES = 36
ROWS = 32
SLOT_ROW = 25
VMEM_BYTES = 40 * 1024 * 1024
F32 = jnp.float32
BF16 = jnp.bfloat16


def lanes(shape):
    return lax.broadcasted_iota(jnp.int32, shape, len(shape) - 1)


def rows(shape):
    return lax.broadcasted_iota(jnp.int32, shape, len(shape) - 2)


def prep_kernel(
    jac_ref, low_ref, high_ref, owner_ref, slot_ref, normals_ref, send_ref, rim_ref, weight_ref, route_ref, wide
):
    faces = owner_ref.shape[0]
    planes = jac_ref.shape[1]
    rim_ref[...] = jnp.zeros_like(rim_ref)
    for c in range(10):
        rim_ref[0, c : c + 1, :] = low_ref[0, c, 0, 0:1, :]
        rim_ref[1, c : c + 1, :] = high_ref[0, c, 0, 7:8, :]

    square = (faces, faces)
    eye = rows(square) == lanes(square)
    owner_col = owner_ref[...].astype(F32)
    owner_row = jnp.sum(jnp.where(eye, owner_col, 0.0), axis=0, keepdims=True)
    slot_col = jnp.sum(jnp.where(eye, slot_ref[...].astype(F32), 0.0), axis=1, keepdims=True)
    earlier = (owner_col == owner_row) & (lanes(square) < rows(square))
    rank = jnp.sum(jnp.where(earlier, 1.0, 0.0), axis=1, keepdims=True)
    route = jnp.where(rows(square).astype(F32) == owner_row, 1.0, 0.0)
    route_ref[...] = route
    lane = lanes((faces, 128))
    table = jnp.where(lane.astype(F32) == rank, slot_col + 1.0, 0.0)
    slots = jnp.dot(route.astype(BF16), table.astype(BF16), preferred_element_type=F32)
    weight = jnp.zeros((faces, 128), F32)
    for d in range(3):
        normal = jnp.sum(jnp.where(eye, normals_ref[d], 0.0), axis=1, keepdims=True)
        hit = ((lane % 8) == d) | ((lane % 8) == d + 3)
        weight = jnp.where(hit, normal, weight)
    weight_ref[...] = jnp.where((lane // 8).astype(F32) == rank, weight, 0.0)

    for e in range(25):
        wide[e * planes : (e + 1) * planes, :] = jac_ref[e].astype(F32)
    wide[SLOT_ROW * planes : (SLOT_ROW + 1) * planes, :] = slots
    wide[(SLOT_ROW + 1) * planes : ROWS * planes, :] = jnp.zeros(((ROWS - SLOT_ROW - 1) * planes, 128), F32)
    for i in range(planes):
        send_ref[i] = wide[pl.ds(i, ROWS, stride=planes), :].astype(BF16)


def sweep_block(b, blocks, passage, phase, u_ref, lo_ref, hi_ref, rim_ref, tile, source_ref, step_ref, diss_ref, freq_ref):
    at = slice(8 * b, 8 * b + 8)
    shape = (8, 128)
    row, lane = rows(shape), lanes(shape)
    u = [u_ref[c, at, :] for c in range(10)]

    def rotated(rim, turn, turned):
        cosine = jnp.where(turned, math.cos(turn), 1.0)
        sine = jnp.where(turned, math.sin(turn), 0.0)
        re = [rim[n] * cosine - rim[5 + n] * sine for n in range(5)]
        im = [rim[n] * sine + rim[5 + n] * cosine for n in range(5)]
        return re + im

    if b == 0:
        before = rotated([rim_ref[1, c : c + 1, :] for c in range(10)], -phase, passage == 0)
    else:
        before = [u_ref[c, 8 * b - 1 : 8 * b, :] for c in range(10)]
    if b == blocks - 1:
        after = rotated([rim_ref[0, c : c + 1, :] for c in range(10)], phase, passage == 1)
    else:
        after = [u_ref[c, 8 * b + 8 : 8 * b + 9, :] for c in range(10)]

    diff = []
    beside = []
    for c in range(10):
        lo, hi = lo_ref[c, at, :], hi_ref[c, at, :]
        diff.append(0.5 * (hi - lo))
        down = jnp.where(row == 0, before[c], pltpu.roll(u[c], 1, axis=0))
        up = jnp.where(row == 7, after[c], pltpu.roll(u[c], 7, axis=0))
        left = jnp.where(lane == 0, 0.0, pltpu.roll(u[c], 1, axis=1))
        right = jnp.where(lane == 127, 0.0, pltpu.roll(u[c], 127, axis=1))
        beside.append(hi + lo + up + down + right + left)
    conv = [None] * 10
    for n in range(5):
        for m in range(5):
            t = tile(5 * n + m)
            re, im = t * diff[n], t * diff[5 + n]
            conv[m] = re if n == 0 else conv[m] + re
            conv[5 + m] = im if n == 0 else conv[5 + m] + im
    step, diss, omega = step_ref[at, :], diss_ref[at, :], freq_ref[at, :]
    new = []
    for c in range(10):
        spin = omega * u[c + 5] if c < 5 else -(omega * u[c - 5])
        resid = conv[c] + spin + diss * (6.0 * u[c] - beside[c]) - source_ref[c, at, :]
        new.append(u[c] - step * resid)
    return new


def first_kernel(
    phase, recv_ref, u_ref, lo_ref, hi_ref, rim_ref, source_ref, step_ref, diss_ref, freq_ref,
    out_ref, tiles_ref, slots_ref, rim_out_ref, wide,
):
    passage = lax.axis_index("passage")
    width = u_ref.shape[1]
    for j in range(width):
        wide[j * ROWS : (j + 1) * ROWS, :] = recv_ref[j].astype(F32)
    slots_ref[...] = wide[pl.ds(SLOT_ROW, width, stride=ROWS), :]
    for e in range(25):
        tiles_ref[e] = wide[pl.ds(e, width, stride=ROWS), :].astype(BF16)
    rim_out_ref[...] = jnp.zeros_like(rim_out_ref)
    blocks = width // 8
    for b in range(blocks):
        new = sweep_block(
            b, blocks, passage, phase, u_ref, lo_ref, hi_ref, rim_ref,
            lambda e: wide[pl.ds(8 * b * ROWS + e, 8, stride=ROWS), :],
            source_ref, step_ref, diss_ref, freq_ref,
        )
        for c in range(10):
            out_ref[c, 8 * b : 8 * b + 8, :] = new[c]
            if b == 0:
                rim_out_ref[0, c : c + 1, :] = new[c][0:1]
            if b == blocks - 1:
                rim_out_ref[1, c : c + 1, :] = new[c][7:8]


def second_kernel(
    phase, tiles_ref, u_ref, lo_ref, hi_ref, rim_ref, source_ref, step_ref, diss_ref, freq_ref, weight_ref, route_ref,
    out_ref, send_ref,
):
    passage = lax.axis_index("passage")
    width = u_ref.shape[1]
    blocks = width // 8
    for b in range(blocks):
        new = sweep_block(
            b, blocks, passage, phase, u_ref, lo_ref, hi_ref, rim_ref,
            lambda e: tiles_ref[e, 8 * b : 8 * b + 8, :].astype(F32),
            source_ref, step_ref, diss_ref, freq_ref,
        )
        for c in range(10):
            out_ref[c, 8 * b : 8 * b + 8, :] = new[c]
    lane = lanes((width, 128)) % 8
    wall = jnp.zeros((width, 128), F32)
    for k, c in enumerate((1, 2, 3, 6, 7, 8)):
        wall = jnp.where(lane == k, out_ref[c, :, 0:1], wall)
    routed = jnp.dot(
        route_ref[...], weight_ref[...] * wall, precision=lax.Precision.HIGHEST, preferred_element_type=F32
    )
    for q in range(send_ref.shape[0]):
        send_ref[q] = routed[q : q + 1, :]


def nodes_kernel(recv_ref, slots_ref, out_ref, dense):
    peers = slots_ref.shape[0]
    for q in range(peers):
        dense[q : q + 1, :] = recv_ref[q]
    total = jnp.zeros((8, NODE_DEV), F32)
    node = lanes((peers, NODE_DEV)).astype(F32) + 1.0
    turned = dense[...].T
    for r in range(CAP):
        hit = jnp.where(slots_ref[:, r : r + 1] == node, 1.0, 0.0)
        total = total + jnp.dot(
            turned[8 * r : 8 * r + 8, :], hit, precision=lax.Precision.HIGHEST, preferred_element_type=F32
        )
    out_ref[...] = total[0:6, :]


def kernel_call(body, out, scratch=(), ins=None):
    options = {} if ins is None else {"grid": (1,), "in_specs": ins[0], "out_specs": ins[1]}
    if ins is None:
        whole = pl.BlockSpec(memory_space=pltpu.VMEM)
        options = {"out_specs": [whole] * len(out)}
    return pl.pallas_call(
        body,
        out_shape=[jax.ShapeDtypeStruct(s, d) for s, d in out],
        scratch_shapes=list(scratch),
        compiler_params=pltpu.CompilerParams(vmem_limit_bytes=VMEM_BYTES),
        **options,
    )


def planes_beside(state, bricks):
    up = [(i, i + 1) for i in range(bricks - 1)]
    down = [(j, i) for i, j in up]
    return lax.ppermute(state, "brick", up), lax.ppermute(state, "brick", down)


def swapped(rim, passes):
    return lax.ppermute(rim, "passage", [(i, (i + 1) % passes) for i in range(passes)])


def body(
    jac_blocks,
    psi_start,
    source,
    pseudo_step,
    dissipation,
    freq_volume,
    normals,
    face_owner,
    face_slot,
):
    passes = lax.axis_size("passage")
    bricks = lax.axis_size("brick")
    width, depth = psi_start.shape[3], psi_start.shape[4]
    phase = 2.0 * math.pi * ND * passes / BLADES
    field = (10, width, depth)
    rim = (2, 16, depth)

    def whole(shape):
        return pl.BlockSpec(shape, lambda _: (0,) * len(shape))

    psi = psi_start.reshape(field)
    jac = jac_blocks.reshape(25, bricks, depth)
    source = source.reshape(field)
    scalars = [a.reshape(width, depth) for a in (pseudo_step, dissipation, freq_volume)]

    lo, hi = planes_beside(psi, bricks)
    edge = (1, 10, 1, 8, depth)
    last = width // 8 - 1
    outs = [((bricks, ROWS, depth), BF16), (rim, F32), ((width, 128), F32), ((bricks, width), F32)]
    send, rims, weight, route = kernel_call(
        prep_kernel,
        outs,
        [pltpu.VMEM((ROWS * bricks, depth), F32)],
        (
            [
                whole(jac.shape),
                pl.BlockSpec(edge, lambda _: (0, 0, 0, 0, 0)),
                pl.BlockSpec(edge, lambda _: (0, 0, 0, last, 0)),
                whole((width, 1)),
                whole((1, width)),
                whole((3, 1, width)),
            ],
            [whole(s) for s, _ in outs],
        ),
    )(jac, psi_start, psi_start, face_owner.reshape(width, 1), face_slot, normals.reshape(3, 1, width))
    recv = lax.all_to_all(send, "brick", 0, 0, tiled=True)
    rims = swapped(rims, passes)

    state, tiles, slots, rims = kernel_call(
        functools.partial(first_kernel, phase),
        [(field, F32), ((25, width, depth), BF16), ((bricks, 128), F32), (rim, F32)],
        [pltpu.VMEM((ROWS * width, depth), F32)],
    )(recv, psi, lo, hi, rims, source, *scalars)

    lo, hi = planes_beside(state, bricks)
    rims = swapped(rims, passes)
    state, routed = kernel_call(
        functools.partial(second_kernel, phase), [(field, F32), ((bricks, 1, 128), F32)]
    )(tiles, state, lo, hi, rims, source, *scalars, weight, route)

    arrived = lax.all_to_all(routed, "brick", 0, 0, tiled=True)
    (sensitivity,) = kernel_call(
        nodes_kernel, [((6, NODE_DEV), F32)], [pltpu.VMEM((bricks, 128), F32)]
    )(arrived, slots)
    return state.reshape(psi_start.shape), sensitivity[None]


def solution(mesh):
    placed = (
        P("passage", None, None, "brick"),
        P("passage", None, "brick", None, None),
        P("passage", None, "brick", None, None),
        P("passage", "brick", None, None),
        P("passage", "brick", None, None),
        P("passage", "brick", None, None),
        P("passage", None, "brick", None),
        P("passage", "brick", None),
        P("passage", "brick"),
    )
    return jax.shard_map(
        body,
        mesh=mesh,
        in_specs=placed,
        out_specs=(P("passage", None, "brick", None, None), P("passage", None, "brick")),
        check_vma=False,
    )
```

```python
import functools
import math

import jax
import jax.numpy as jnp
from jax import lax
from jax.experimental import pallas as pl
from jax.experimental.pallas import tpu as pltpu
from jax.sharding import PartitionSpec as P

NODE_DEV = 256
CAP = 4
ND = 1
BLADES = 36
ROWS = 32
BLOCK = 16
FULL = 32000.0
VMEM_BYTES = 40 * 1024 * 1024
F32 = jnp.float32
BF16 = jnp.bfloat16
I16 = jnp.int16


def lanes(shape):
    return lax.broadcasted_iota(jnp.int32, shape, len(shape) - 1)


def rows(shape):
    return lax.broadcasted_iota(jnp.int32, shape, len(shape) - 2)


def prep_kernel(jac_ref, send_ref, wide):
    planes = jac_ref.shape[1]
    wide[25 * planes : ROWS * planes, :] = jnp.zeros(((ROWS - 25) * planes, 128), F32)
    for e in range(25):
        wide[e * planes : (e + 1) * planes, :] = jac_ref[e].astype(F32)
    for i in range(planes):
        send_ref[i] = wide[pl.ds(i, ROWS, stride=planes), :].astype(BF16)


def aux_kernel(psi_ref, owner_ref, slot_ref, normals_ref, rim_ref, weight_ref, route_ref, code_ref):
    width = psi_ref.shape[1]
    faces = owner_ref.shape[1]
    coded(psi_ref, code_ref)
    rim_ref[...] = jnp.zeros_like(rim_ref)
    for c in range(10):
        rim_ref[0, c : c + 1, :] = psi_ref[c, 0:1, :]
        rim_ref[1, c : c + 1, :] = psi_ref[c, width - 1 : width, :]

    square = (faces, faces)
    eye = rows(square) == lanes(square)

    def column(row):
        return jnp.sum(jnp.where(eye, row, 0.0), axis=1, keepdims=True)

    owner_row = owner_ref[...].astype(F32)
    owner_col = column(owner_row)
    slot_col = column(slot_ref[...].astype(F32))
    earlier = (owner_col == owner_row) & (lanes(square) < rows(square))
    rank = jnp.sum(jnp.where(earlier, 1.0, 0.0), axis=1, keepdims=True)
    route_ref[...] = jnp.where(rows(square).astype(F32) == owner_row, 1.0, 0.0)
    lane = lanes((faces, 128))
    weight = jnp.where(lane % 8 == 6, slot_col + 1.0, 0.0)
    for d in range(3):
        hit = ((lane % 8) == d) | ((lane % 8) == d + 3)
        weight = jnp.where(hit, column(normals_ref[d]), weight)
    weight_ref[...] = jnp.where((lane // 8).astype(F32) == rank, weight, 0.0)


def coded(u_ref, code_ref):
    width = u_ref.shape[1]
    exponents = jnp.zeros((16, 128), F32)
    row = rows((16, 128))
    for c in range(10):
        top = jnp.max(jnp.abs(u_ref[c]), axis=0, keepdims=True)
        top = jnp.max(top, axis=1, keepdims=True)
        exponent = jnp.ceil(jnp.log2(jnp.maximum(top, 1e-30)))
        code_ref[c * width : (c + 1) * width, :] = jnp.round(u_ref[c] * (FULL * jnp.exp2(-exponent))).astype(jnp.int32).astype(I16)
        exponents = jnp.where(row == c, exponent, exponents)
    code_ref[10 * width :, :] = exponents.astype(jnp.int32).astype(I16)


def code_scale(code_ref):
    exponents = code_ref[code_ref.shape[0] - 16 :, :].astype(jnp.int32).astype(F32)
    scale = jnp.exp2(exponents) * (1.0 / FULL)
    return [scale[c : c + 1, :] for c in range(10)]


def sweep_block(b, blocks, passage, phase, u_ref, lo_ref, hi_ref, scales, rim_ref, tile, source_ref, step_ref, diss_ref, freq_ref):
    at = slice(BLOCK * b, BLOCK * b + BLOCK)
    shape = (BLOCK, 128)
    row, lane = rows(shape), lanes(shape)
    width = u_ref.shape[1]
    u = [u_ref[c, at, :] for c in range(10)]

    def rotated(rim, turn, turned):
        cosine = jnp.where(turned, math.cos(turn), 1.0)
        sine = jnp.where(turned, math.sin(turn), 0.0)
        re = [rim[n] * cosine - rim[5 + n] * sine for n in range(5)]
        im = [rim[n] * sine + rim[5 + n] * cosine for n in range(5)]
        return re + im

    if b == 0:
        before = rotated([rim_ref[1, c : c + 1, :] for c in range(10)], -phase, passage == 0)
    else:
        before = [u_ref[c, BLOCK * b - 1 : BLOCK * b, :] for c in range(10)]
    if b == blocks - 1:
        after = rotated([rim_ref[0, c : c + 1, :] for c in range(10)], phase, passage == 1)
    else:
        after = [u_ref[c, BLOCK * b + BLOCK : BLOCK * b + BLOCK + 1, :] for c in range(10)]

    diff = []
    beside = []
    for c in range(10):
        first = c * width + BLOCK * b
        lo = lo_ref[first : first + BLOCK, :].astype(jnp.int32).astype(F32) * scales[0][c]
        hi = hi_ref[first : first + BLOCK, :].astype(jnp.int32).astype(F32) * scales[1][c]
        diff.append(0.5 * (hi - lo))
        down = jnp.where(row == 0, before[c], pltpu.roll(u[c], 1, axis=0))
        up = jnp.where(row == BLOCK - 1, after[c], pltpu.roll(u[c], BLOCK - 1, axis=0))
        left = jnp.where(lane == 0, 0.0, pltpu.roll(u[c], 1, axis=1))
        right = jnp.where(lane == 127, 0.0, pltpu.roll(u[c], 127, axis=1))
        beside.append(hi + lo + up + down + right + left)
    conv = [None] * 10
    for n in range(5):
        for m in range(5):
            t = tile(5 * n + m)
            re, im = t * diff[n], t * diff[5 + n]
            conv[m] = re if n == 0 else conv[m] + re
            conv[5 + m] = im if n == 0 else conv[5 + m] + im
    step, diss, omega = step_ref[at, :], diss_ref[at, :], freq_ref[at, :]
    new = []
    for c in range(10):
        spin = omega * u[c + 5] if c < 5 else -(omega * u[c - 5])
        resid = conv[c] + spin + diss * (6.0 * u[c] - beside[c]) - source_ref[c, at, :]
        new.append(u[c] - step * resid)
    return new


def first_kernel(
    phase, recv_ref, u_ref, lo_ref, hi_ref, rim_ref, source_ref, step_ref, diss_ref, freq_ref,
    out_ref, tiles_ref, rim_out_ref, code_ref, wide,
):
    passage = lax.axis_index("passage")
    width = u_ref.shape[1]
    for j in range(width):
        wide[j * ROWS : (j + 1) * ROWS, :] = recv_ref[j].astype(F32)
    for e in range(25):
        tiles_ref[e] = wide[pl.ds(e, width, stride=ROWS), :].astype(BF16)
    rim_out_ref[...] = jnp.zeros_like(rim_out_ref)
    blocks = width // BLOCK
    scales = code_scale(lo_ref), code_scale(hi_ref)
    for b in range(blocks):
        new = sweep_block(
            b, blocks, passage, phase, u_ref, lo_ref, hi_ref, scales, rim_ref,
            lambda e: wide[pl.ds(BLOCK * b * ROWS + e, BLOCK, stride=ROWS), :],
            source_ref, step_ref, diss_ref, freq_ref,
        )
        for c in range(10):
            out_ref[c, BLOCK * b : BLOCK * b + BLOCK, :] = new[c]
            if b == 0:
                rim_out_ref[0, c : c + 1, :] = new[c][0:1]
            if b == blocks - 1:
                rim_out_ref[1, c : c + 1, :] = new[c][BLOCK - 1 : BLOCK]
    coded(out_ref, code_ref)


def second_kernel(
    phase, tiles_ref, u_ref, lo_ref, hi_ref, rim_ref, source_ref, step_ref, diss_ref, freq_ref, weight_ref, route_ref,
    out_ref, send_ref,
):
    passage = lax.axis_index("passage")
    width = u_ref.shape[1]
    blocks = width // BLOCK
    scales = code_scale(lo_ref), code_scale(hi_ref)
    for b in range(blocks):
        new = sweep_block(
            b, blocks, passage, phase, u_ref, lo_ref, hi_ref, scales, rim_ref,
            lambda e: tiles_ref[e, BLOCK * b : BLOCK * b + BLOCK, :].astype(F32),
            source_ref, step_ref, diss_ref, freq_ref,
        )
        for c in range(10):
            out_ref[c, BLOCK * b : BLOCK * b + BLOCK, :] = new[c]
    lane = lanes((width, 128)) % 8
    wall = jnp.ones((width, 128), F32)
    for k, c in enumerate((1, 2, 3, 6, 7, 8)):
        wall = jnp.where(lane == k, out_ref[c, :, 0:1], wall)
    routed = jnp.dot(
        route_ref[...], weight_ref[...] * wall, precision=lax.Precision.HIGHEST, preferred_element_type=F32
    )
    for q in range(send_ref.shape[0]):
        send_ref[q] = routed[q : q + 1, :]


def nodes_kernel(recv_ref, out_ref, dense):
    peers = recv_ref.shape[0]
    for q in range(peers):
        dense[q : q + 1, :] = recv_ref[q]
    total = jnp.zeros((8, NODE_DEV), F32)
    node = lanes((peers, NODE_DEV)).astype(F32) + 1.0
    turned = dense[...].T
    for r in range(CAP):
        hit = jnp.where(dense[:, 8 * r + 6 : 8 * r + 7] == node, 1.0, 0.0)
        total = total + jnp.dot(
            turned[8 * r : 8 * r + 8, :], hit, precision=lax.Precision.HIGHEST, preferred_element_type=F32
        )
    out_ref[...] = total[0:6, :]


def kernel_call(body, out, scratch=()):
    whole = pl.BlockSpec(memory_space=pltpu.VMEM)
    return pl.pallas_call(
        body,
        out_shape=[jax.ShapeDtypeStruct(s, d) for s, d in out],
        out_specs=[whole] * len(out),
        scratch_shapes=list(scratch),
        compiler_params=pltpu.CompilerParams(vmem_limit_bytes=VMEM_BYTES),
    )


def planes_beside(state, bricks):
    up = [(i, i + 1) for i in range(bricks - 1)]
    down = [(j, i) for i, j in up]
    return lax.ppermute(state, "brick", up), lax.ppermute(state, "brick", down)


def swapped(rim, passes):
    return lax.ppermute(rim, "passage", [(i, (i + 1) % passes) for i in range(passes)])


def body(
    jac_blocks,
    psi_start,
    source,
    pseudo_step,
    dissipation,
    freq_volume,
    normals,
    face_owner,
    face_slot,
):
    passes = lax.axis_size("passage")
    bricks = lax.axis_size("brick")
    width, depth = psi_start.shape[3], psi_start.shape[4]
    phase = 2.0 * math.pi * ND * passes / BLADES
    field = (10, width, depth)
    rim = (2, 16, depth)
    plane = (10 * width + 16, depth)

    psi = psi_start.reshape(field)
    jac = jac_blocks.reshape(25, bricks, depth)
    source = source.reshape(field)
    scalars = [a.reshape(width, depth) for a in (pseudo_step, dissipation, freq_volume)]

    (send,) = kernel_call(
        prep_kernel,
        [((bricks, ROWS, depth), BF16)],
        [pltpu.VMEM((ROWS * bricks, depth), F32)],
    )(jac)
    recv = lax.all_to_all(send, "brick", 0, 0, tiled=True)
    rims, weight, route, code = kernel_call(
        aux_kernel, [(rim, F32), ((width, 128), F32), ((bricks, width), F32), (plane, I16)]
    )(psi, face_owner.reshape(1, width), face_slot, normals.reshape(3, 1, width))
    lo, hi = planes_beside(code, bricks)
    rims = swapped(rims, passes)

    state, tiles, rims, code = kernel_call(
        functools.partial(first_kernel, phase),
        [(field, F32), ((25, width, depth), BF16), (rim, F32), (plane, I16)],
        [pltpu.VMEM((ROWS * width, depth), F32)],
    )(recv, psi, lo, hi, rims, source, *scalars)

    lo, hi = planes_beside(code, bricks)
    rims = swapped(rims, passes)
    state, routed = kernel_call(
        functools.partial(second_kernel, phase), [(field, F32), ((bricks, 1, 128), F32)]
    )(tiles, state, lo, hi, rims, source, *scalars, weight, route)

    arrived = lax.all_to_all(routed, "brick", 0, 0, tiled=True)
    (sensitivity,) = kernel_call(
        nodes_kernel, [((6, NODE_DEV), F32)], [pltpu.VMEM((bricks, 128), F32)]
    )(arrived)
    return state.reshape(psi_start.shape), sensitivity[None]


def solution(mesh):
    placed = (
        P("passage", None, None, "brick"),
        P("passage", None, "brick", None, None),
        P("passage", None, "brick", None, None),
        P("passage", "brick", None, None),
        P("passage", "brick", None, None),
        P("passage", "brick", None, None),
        P("passage", None, "brick", None),
        P("passage", "brick", None),
        P("passage", "brick"),
    )
    return jax.shard_map(
        body,
        mesh=mesh,
        in_specs=placed,
        out_specs=(P("passage", None, "brick", None, None), P("passage", None, "brick")),
        check_vma=False,
    )
```

```python
import functools
import math

import jax
import jax.numpy as jnp
from jax import lax
from jax.experimental import pallas as pl
from jax.experimental.pallas import tpu as pltpu
from jax.sharding import PartitionSpec as P

NODE_DEV = 256
CAP = 4
ND = 1
BLADES = 36
ROWS = 32
BLOCK = 16
FULL = 32000.0
VMEM_BYTES = 40 * 1024 * 1024
F32 = jnp.float32
BF16 = jnp.bfloat16
I16 = jnp.int16


def lanes(shape):
    return lax.broadcasted_iota(jnp.int32, shape, len(shape) - 1)


def rows(shape):
    return lax.broadcasted_iota(jnp.int32, shape, len(shape) - 2)


def prep_kernel(jac_ref, send_ref, wide):
    planes = jac_ref.shape[1]
    wide[25 * planes : ROWS * planes, :] = jnp.zeros(((ROWS - 25) * planes, 128), F32)
    for e in range(25):
        wide[e * planes : (e + 1) * planes, :] = jac_ref[e].astype(F32)
    for i in range(planes):
        send_ref[i] = wide[pl.ds(i, ROWS, stride=planes), :].astype(BF16)


def aux_kernel(psi_ref, owner_ref, slot_ref, normals_ref, rim_ref, weight_ref, route_ref, code_ref):
    width = psi_ref.shape[1]
    faces = owner_ref.shape[1]
    coded(psi_ref, code_ref)
    rim_ref[...] = jnp.zeros_like(rim_ref)
    for c in range(10):
        rim_ref[0, c : c + 1, :] = psi_ref[c, 0:1, :]
        rim_ref[1, c : c + 1, :] = psi_ref[c, width - 1 : width, :]

    square = (faces, faces)
    eye = rows(square) == lanes(square)

    def column(row):
        return jnp.sum(jnp.where(eye, row, 0.0), axis=1, keepdims=True)

    owner_row = owner_ref[...].astype(F32)
    owner_col = column(owner_row)
    slot_col = column(slot_ref[...].astype(F32))
    earlier = (owner_col == owner_row) & (lanes(square) < rows(square))
    rank = jnp.sum(jnp.where(earlier, 1.0, 0.0), axis=1, keepdims=True)
    route_ref[...] = jnp.where(rows(square).astype(F32) == owner_row, 1.0, 0.0)
    lane = lanes((faces, 128))
    weight = jnp.where(lane % 8 == 6, slot_col + 1.0, 0.0)
    for d in range(3):
        hit = ((lane % 8) == d) | ((lane % 8) == d + 3)
        weight = jnp.where(hit, column(normals_ref[d]), weight)
    weight_ref[...] = jnp.where((lane // 8).astype(F32) == rank, weight, 0.0)


def coded(u_ref, code_ref):
    width = u_ref.shape[1]
    exponents = jnp.zeros((16, 128), F32)
    row = rows((16, 128))
    for c in range(10):
        top = jnp.max(jnp.abs(u_ref[c]), axis=0, keepdims=True)
        top = jnp.max(top, axis=1, keepdims=True)
        exponent = jnp.ceil(jnp.log2(jnp.maximum(top, 1e-30)))
        code_ref[c * width : (c + 1) * width, :] = jnp.round(u_ref[c] * (FULL * jnp.exp2(-exponent))).astype(jnp.int32).astype(I16)
        exponents = jnp.where(row == c, exponent, exponents)
    code_ref[10 * width :, :] = exponents.astype(jnp.int32).astype(I16)


def code_scale(code_ref):
    exponents = code_ref[code_ref.shape[0] - 16 :, :].astype(jnp.int32).astype(F32)
    scale = jnp.exp2(exponents) * (1.0 / FULL)
    return [scale[c : c + 1, :] for c in range(10)]


def sweep_block(b, blocks, passage, phase, u_ref, near_ref, far_ref, scales, rim_ref, tile, source_ref, step_ref, diss_ref, freq_ref):
    at = slice(BLOCK * b, BLOCK * b + BLOCK)
    shape = (BLOCK, 128)
    row, lane = rows(shape), lanes(shape)
    width = u_ref.shape[1]
    u = [u_ref[c, at, :] for c in range(10)]

    def rotated(rim, turn, turned):
        cosine = jnp.where(turned, math.cos(turn), 1.0)
        sine = jnp.where(turned, math.sin(turn), 0.0)
        re = [rim[n] * cosine - rim[5 + n] * sine for n in range(5)]
        im = [rim[n] * sine + rim[5 + n] * cosine for n in range(5)]
        return re + im

    if b == 0:
        before = rotated([rim_ref[1, c : c + 1, :] for c in range(10)], -phase, passage == 0)
    else:
        before = [u_ref[c, BLOCK * b - 1 : BLOCK * b, :] for c in range(10)]
    if b == blocks - 1:
        after = rotated([rim_ref[0, c : c + 1, :] for c in range(10)], phase, passage == 1)
    else:
        after = [u_ref[c, BLOCK * b + BLOCK : BLOCK * b + BLOCK + 1, :] for c in range(10)]

    half = jnp.where(lax.axis_index("brick") % 2 == 0, 0.5, -0.5)
    diff = []
    beside = []
    for c in range(10):
        first = c * width + BLOCK * b
        near = near_ref[first : first + BLOCK, :].astype(jnp.int32).astype(F32) * scales[0][c]
        far = far_ref[first : first + BLOCK, :].astype(jnp.int32).astype(F32) * scales[1][c]
        diff.append(half * (near - far))
        down = jnp.where(row == 0, before[c], pltpu.roll(u[c], 1, axis=0))
        up = jnp.where(row == BLOCK - 1, after[c], pltpu.roll(u[c], BLOCK - 1, axis=0))
        left = jnp.where(lane == 0, 0.0, pltpu.roll(u[c], 1, axis=1))
        right = jnp.where(lane == 127, 0.0, pltpu.roll(u[c], 127, axis=1))
        beside.append(near + far + up + down + right + left)
    conv = [None] * 10
    for n in range(5):
        for m in range(5):
            t = tile(5 * n + m)
            re, im = t * diff[n], t * diff[5 + n]
            conv[m] = re if n == 0 else conv[m] + re
            conv[5 + m] = im if n == 0 else conv[5 + m] + im
    step, diss, omega = step_ref[at, :], diss_ref[at, :], freq_ref[at, :]
    new = []
    for c in range(10):
        spin = omega * u[c + 5] if c < 5 else -(omega * u[c - 5])
        resid = conv[c] + spin + diss * (6.0 * u[c] - beside[c]) - source_ref[c, at, :]
        new.append(u[c] - step * resid)
    return new


def first_kernel(
    phase, recv_ref, u_ref, near_ref, far_ref, rim_ref, source_ref, step_ref, diss_ref, freq_ref,
    out_ref, tiles_ref, rim_out_ref, code_ref, wide,
):
    passage = lax.axis_index("passage")
    width = u_ref.shape[1]
    for j in range(width):
        wide[j * ROWS : (j + 1) * ROWS, :] = recv_ref[j].astype(F32)
    for e in range(25):
        tiles_ref[e] = wide[pl.ds(e, width, stride=ROWS), :].astype(BF16)
    rim_out_ref[...] = jnp.zeros_like(rim_out_ref)
    blocks = width // BLOCK
    scales = code_scale(near_ref), code_scale(far_ref)
    for b in range(blocks):
        new = sweep_block(
            b, blocks, passage, phase, u_ref, near_ref, far_ref, scales, rim_ref,
            lambda e: wide[pl.ds(BLOCK * b * ROWS + e, BLOCK, stride=ROWS), :],
            source_ref, step_ref, diss_ref, freq_ref,
        )
        for c in range(10):
            out_ref[c, BLOCK * b : BLOCK * b + BLOCK, :] = new[c]
            if b == 0:
                rim_out_ref[0, c : c + 1, :] = new[c][0:1]
            if b == blocks - 1:
                rim_out_ref[1, c : c + 1, :] = new[c][BLOCK - 1 : BLOCK]
    coded(out_ref, code_ref)


def second_kernel(
    phase, tiles_ref, u_ref, near_ref, far_ref, rim_ref, source_ref, step_ref, diss_ref, freq_ref, weight_ref, route_ref,
    out_ref, send_ref,
):
    passage = lax.axis_index("passage")
    width = u_ref.shape[1]
    blocks = width // BLOCK
    scales = code_scale(near_ref), code_scale(far_ref)
    for b in range(blocks):
        new = sweep_block(
            b, blocks, passage, phase, u_ref, near_ref, far_ref, scales, rim_ref,
            lambda e: tiles_ref[e, BLOCK * b : BLOCK * b + BLOCK, :].astype(F32),
            source_ref, step_ref, diss_ref, freq_ref,
        )
        for c in range(10):
            out_ref[c, BLOCK * b : BLOCK * b + BLOCK, :] = new[c]
    lane = lanes((width, 128)) % 8
    wall = jnp.ones((width, 128), F32)
    for k, c in enumerate((1, 2, 3, 6, 7, 8)):
        wall = jnp.where(lane == k, out_ref[c, :, 0:1], wall)
    routed = jnp.dot(
        route_ref[...], weight_ref[...] * wall, precision=lax.Precision.HIGHEST, preferred_element_type=F32
    )
    for q in range(send_ref.shape[0]):
        send_ref[q] = routed[q : q + 1, :]


def nodes_kernel(recv_ref, out_ref, dense):
    peers = recv_ref.shape[0]
    for q in range(peers):
        dense[q : q + 1, :] = recv_ref[q]
    total = jnp.zeros((8, NODE_DEV), F32)
    node = lanes((peers, NODE_DEV)).astype(F32) + 1.0
    turned = dense[...].T
    for r in range(CAP):
        hit = jnp.where(dense[:, 8 * r + 6 : 8 * r + 7] == node, 1.0, 0.0)
        total = total + jnp.dot(
            turned[8 * r : 8 * r + 8, :], hit, precision=lax.Precision.HIGHEST, preferred_element_type=F32
        )
    out_ref[...] = total[0:6, :]


def kernel_call(body, out, scratch=()):
    whole = pl.BlockSpec(memory_space=pltpu.VMEM)
    return pl.pallas_call(
        body,
        out_shape=[jax.ShapeDtypeStruct(s, d) for s, d in out],
        out_specs=[whole] * len(out),
        scratch_shapes=list(scratch),
        compiler_params=pltpu.CompilerParams(vmem_limit_bytes=VMEM_BYTES),
    )


def planes_beside(code, bricks):
    near = [(i, i ^ 1) for i in range(bricks)]
    far = [(i, i - 1 if i % 2 == 0 else i + 1) for i in range(1, bricks - 1)]
    return lax.ppermute(code, "brick", near), lax.ppermute(code, "brick", far)


def swapped(rim, passes):
    return lax.ppermute(rim, "passage", [(i, (i + 1) % passes) for i in range(passes)])


def body(
    jac_blocks,
    psi_start,
    source,
    pseudo_step,
    dissipation,
    freq_volume,
    normals,
    face_owner,
    face_slot,
):
    passes = lax.axis_size("passage")
    bricks = lax.axis_size("brick")
    width, depth = psi_start.shape[3], psi_start.shape[4]
    phase = 2.0 * math.pi * ND * passes / BLADES
    field = (10, width, depth)
    rim = (2, 16, depth)
    plane = (10 * width + 16, depth)

    psi = psi_start.reshape(field)
    jac = jac_blocks.reshape(25, bricks, depth)
    source = source.reshape(field)
    scalars = [a.reshape(width, depth) for a in (pseudo_step, dissipation, freq_volume)]

    (send,) = kernel_call(
        prep_kernel,
        [((bricks, ROWS, depth), BF16)],
        [pltpu.VMEM((ROWS * bricks, depth), F32)],
    )(jac)
    recv = lax.all_to_all(send, "brick", 0, 0, tiled=True)
    rims, weight, route, code = kernel_call(
        aux_kernel, [(rim, F32), ((width, 128), F32), ((bricks, width), F32), (plane, I16)]
    )(psi, face_owner.reshape(1, width), face_slot, normals.reshape(3, 1, width))
    near, far = planes_beside(code, bricks)
    rims = swapped(rims, passes)

    state, tiles, rims, code = kernel_call(
        functools.partial(first_kernel, phase),
        [(field, F32), ((25, width, depth), BF16), (rim, F32), (plane, I16)],
        [pltpu.VMEM((ROWS * width, depth), F32)],
    )(recv, psi, near, far, rims, source, *scalars)

    near, far = planes_beside(code, bricks)
    rims = swapped(rims, passes)
    state, routed = kernel_call(
        functools.partial(second_kernel, phase), [(field, F32), ((bricks, 1, 128), F32)]
    )(tiles, state, near, far, rims, source, *scalars, weight, route)

    arrived = lax.all_to_all(routed, "brick", 0, 0, tiled=True)
    (sensitivity,) = kernel_call(
        nodes_kernel, [((6, NODE_DEV), F32)], [pltpu.VMEM((bricks, 128), F32)]
    )(arrived)
    return state.reshape(psi_start.shape), sensitivity[None]


def solution(mesh):
    placed = (
        P("passage", None, None, "brick"),
        P("passage", None, "brick", None, None),
        P("passage", None, "brick", None, None),
        P("passage", "brick", None, None),
        P("passage", "brick", None, None),
        P("passage", "brick", None, None),
        P("passage", None, "brick", None),
        P("passage", "brick", None),
        P("passage", "brick"),
    )
    return jax.shard_map(
        body,
        mesh=mesh,
        in_specs=placed,
        out_specs=(P("passage", None, "brick", None, None), P("passage", None, "brick")),
        check_vma=False,
    )
```

```python
import functools
import math

import jax
import jax.numpy as jnp
from jax import lax
from jax.experimental import pallas as pl
from jax.experimental.pallas import tpu as pltpu
from jax.sharding import PartitionSpec as P

NODE_DEV = 256
CAP = 4
PLANES = 3
WALL = (1, 2, 3, 6, 7, 8)
ND = 1
BLADES = 36
ROWS = 32
BLOCK = 16
FULL = 32000.0
AHEAD = 1 << 34
VMEM_BYTES = 40 * 1024 * 1024
F32 = jnp.float32
BF16 = jnp.bfloat16
I16 = jnp.int16


def lanes(shape):
    return lax.broadcasted_iota(jnp.int32, shape, len(shape) - 1)


def rows(shape):
    return lax.broadcasted_iota(jnp.int32, shape, len(shape) - 2)


def prep_kernel(jac_ref, send_ref, wide):
    planes = jac_ref.shape[1]
    wide[25 * planes : ROWS * planes, :] = jnp.zeros(((ROWS - 25) * planes, 128), F32)
    lane = lanes((planes, 128))
    wall = jnp.zeros((planes, 128), F32)
    for e in range(25):
        entry = jac_ref[e].astype(F32)
        wide[e * planes : (e + 1) * planes, :] = entry
        wall = jnp.where(lane == e, pltpu.roll(entry, e, axis=1) if e else entry, wall)
    wide[25 * planes + 1 : 26 * planes, :] = wall[0 : planes - 1]
    wide[26 * planes : 27 * planes - 1, :] = wall[1:planes]
    for i in range(planes):
        send_ref[i] = wide[pl.ds(i, ROWS, stride=planes), :].astype(BF16)


def routing(owner_row, rank, values, first):
    faces = rank.shape[0]
    square = (faces, faces)
    lane = lanes((faces, 128))
    within = lane % 8
    weight = jnp.where(within == 6, values[3], 0.0)
    for d in range(3):
        weight = jnp.where((within == d) | (within == d + 3), values[d], weight)
    weight = jnp.where((lane // 8 - first).astype(F32) == rank, weight, 0.0)
    return jnp.where(rows(square).astype(F32) == owner_row, 1.0, 0.0), weight


def turned(value):
    length = max(value.shape)
    square = (length, length)
    eye = rows(square) == lanes(square)
    return jnp.sum(jnp.where(eye, value, 0.0), axis=1 if value.shape[0] == 1 else 0, keepdims=True)


def aux_kernel(
    psi_ref, source_ref, step_ref, diss_ref, freq_ref, owner_ref, slot_ref, normals_ref,
    rim_ref, weight_ref, route_ref, code_ref, fields_ref,
):
    width = psi_ref.shape[1]
    rim_ref[...] = jnp.zeros_like(rim_ref)
    for c in range(10):
        rim_ref[0, c : c + 1, :] = psi_ref[c, 0:1, :]
        rim_ref[1, c : c + 1, :] = psi_ref[c, width - 1 : width, :]

    square = (width, width)
    owner_row = owner_ref[...].astype(F32)
    owner = turned(owner_row)
    slot = turned(slot_ref[...].astype(F32)) + 1.0
    earlier = (owner == owner_row) & (lanes(square) < rows(square))
    rank = jnp.sum(jnp.where(earlier, 1.0, 0.0), axis=1, keepdims=True)
    normals = [turned(normals_ref[d]) for d in range(3)]
    route_ref[...], weight_ref[...] = routing(owner_row, rank, normals + [slot], 0)

    step, diss, omega = step_ref[:, 0:1], diss_ref[:, 0:1], freq_ref[:, 0:1]
    lane = lanes((width, 128))
    info = jnp.zeros((width, 128), F32)
    for k, value in enumerate([step * n for n in normals] + [slot, diss, owner, rank]):
        info = jnp.where(lane == k, value, info)
    coded(psi_ref, code_ref, info)

    within = lane % 8
    flow = jnp.zeros((width, 128), F32)
    for k, c in enumerate(WALL):
        flow = jnp.where(within == k, source_ref[c, :, 0:1], flow)
    fields_ref[0] = jnp.zeros((width, 128), F32) + step
    fields_ref[1] = jnp.zeros((width, 128), F32) + diss
    fields_ref[2] = jnp.where(within < 3, omega, -omega)
    fields_ref[3] = flow


def beside_kernel(near_ref, far_ref, weight_ref, route_ref, diss_ref):
    width = weight_ref.shape[1]
    for at, ref in enumerate((near_ref, far_ref)):
        last = ref.shape[0] - width
        exponent = ref[last - 16 : last, :].astype(jnp.int32).astype(F32)[15:16, :]
        code = ref[last:, :].astype(jnp.int32).astype(F32)
        low = pltpu.roll(code, 120, axis=1)
        info = (code + low * (1.0 / FULL)) * (jnp.exp2(exponent) * (1.0 / FULL))
        column = [info[:, k : k + 1] for k in range(7)]
        slot, owner, rank = [jnp.round(column[k]) for k in (3, 5, 6)]
        route_ref[at], weight_ref[at] = routing(turned(owner), rank, column[:3] + [slot], CAP * (at + 1))
        diss_ref[at] = jnp.zeros((width, 128), F32) + column[4]


def exponent_of(top):
    return jnp.ceil(jnp.log2(jnp.maximum(top, 1e-30)))


def short(value):
    return jnp.round(value).astype(jnp.int32).astype(I16)


def coded(u_ref, code_ref, info=None):
    width = u_ref.shape[1]
    exponents = jnp.zeros((16, 128), F32)
    row = rows((16, 128))
    for c in range(10):
        top = jnp.max(jnp.abs(u_ref[c]), axis=0, keepdims=True)
        top = jnp.max(top, axis=1, keepdims=True)
        exponent = exponent_of(top)
        code_ref[c * width : (c + 1) * width, :] = short(u_ref[c] * (FULL * jnp.exp2(-exponent)))
        exponents = jnp.where(row == c, exponent, exponents)
    if info is not None:
        exponent = exponent_of(jnp.max(jnp.abs(info), axis=0, keepdims=True))
        exponents = jnp.where(row == 15, exponent, exponents)
        value = info * (FULL * jnp.exp2(-exponent))
        high = jnp.round(value)
        low = jnp.round((value - high) * FULL)
        lane = lanes((width, 128))
        both = jnp.where(lane < 8, high, jnp.where(lane < 16, pltpu.roll(low, 8, axis=1), 0.0))
        code_ref[10 * width + 16 :, :] = short(both)
    code_ref[10 * width : 10 * width + 16, :] = short(exponents)


def code_scale(code_ref, width):
    exponents = code_ref[10 * width : 10 * width + 16, :].astype(jnp.int32).astype(F32)
    scale = jnp.exp2(exponents) * (1.0 / FULL)
    return [scale[c : c + 1, :] for c in range(10)]


def rims_beside(rim_ref, passage, phase):
    def rotated(at, turn, edge):
        cosine = jnp.where(passage == edge, math.cos(turn), 1.0)
        sine = jnp.where(passage == edge, math.sin(turn), 0.0)
        rim = [rim_ref[at, c : c + 1, :] for c in range(10)]
        re = [rim[n] * cosine - rim[5 + n] * sine for n in range(5)]
        im = [rim[n] * sine + rim[5 + n] * cosine for n in range(5)]
        return re + im

    return rotated(1, -phase, 0), rotated(0, phase, 1)


def sweep_block(b, blocks, u_ref, near_ref, far_ref, scales, rims, tile, source_ref, step_ref, diss_ref, freq_ref):
    at = slice(BLOCK * b, BLOCK * b + BLOCK)
    shape = (BLOCK, 128)
    row, lane = rows(shape), lanes(shape)
    width = u_ref.shape[1]
    u = [u_ref[c, at, :] for c in range(10)]

    if b == 0:
        before = rims[0]
    else:
        before = [u_ref[c, BLOCK * b - 1 : BLOCK * b, :] for c in range(10)]
    if b == blocks - 1:
        after = rims[1]
    else:
        after = [u_ref[c, BLOCK * b + BLOCK : BLOCK * b + BLOCK + 1, :] for c in range(10)]

    half = jnp.where(lax.axis_index("brick") % 2 == 0, 0.5, -0.5)
    diff = []
    beside = []
    for c in range(10):
        first = c * width + BLOCK * b
        near = near_ref[first : first + BLOCK, :].astype(jnp.int32).astype(F32) * scales[0][c]
        far = far_ref[first : first + BLOCK, :].astype(jnp.int32).astype(F32) * scales[1][c]
        diff.append(half * (near - far))
        down = jnp.where(row == 0, before[c], pltpu.roll(u[c], 1, axis=0))
        up = jnp.where(row == BLOCK - 1, after[c], pltpu.roll(u[c], BLOCK - 1, axis=0))
        left = jnp.where(lane == 0, 0.0, pltpu.roll(u[c], 1, axis=1))
        right = jnp.where(lane == 127, 0.0, pltpu.roll(u[c], 127, axis=1))
        beside.append(near + far + up + down + right + left)
    conv = [None] * 10
    for n in range(5):
        for m in range(5):
            t = tile(5 * n + m)
            re, im = t * diff[n], t * diff[5 + n]
            conv[m] = re if n == 0 else conv[m] + re
            conv[5 + m] = im if n == 0 else conv[5 + m] + im
    step, diss, omega = step_ref[at, :], diss_ref[at, :], freq_ref[at, :]
    new = []
    for c in range(10):
        spin = omega * u[c + 5] if c < 5 else -(omega * u[c - 5])
        resid = conv[c] + spin + diss * (6.0 * u[c] - beside[c]) - source_ref[c, at, :]
        new.append(u[c] - step * resid)
    return new


def first_kernel(
    phase, recv_ref, u_ref, near_ref, far_ref, rim_ref, source_ref, step_ref, diss_ref, freq_ref,
    out_ref, tiles_ref, rim_out_ref, code_ref, walls_ref, wide,
):
    rims = rims_beside(rim_ref, lax.axis_index("passage"), phase)
    width = u_ref.shape[1]
    for j in range(width):
        wide[j * ROWS : (j + 1) * ROWS, :] = recv_ref[j].astype(F32)
    for at in range(2):
        walls_ref[at] = wide[pl.ds(25 + at, width, stride=ROWS), :]
    for e in range(25):
        tiles_ref[e] = wide[pl.ds(e, width, stride=ROWS), :].astype(BF16)
    rim_out_ref[...] = jnp.zeros_like(rim_out_ref)
    blocks = width // BLOCK
    scales = code_scale(near_ref, width), code_scale(far_ref, width)
    for b in range(blocks):
        new = sweep_block(
            b, blocks, u_ref, near_ref, far_ref, scales, rims,
            lambda e: wide[pl.ds(BLOCK * b * ROWS + e, BLOCK, stride=ROWS), :],
            source_ref, step_ref, diss_ref, freq_ref,
        )
        for c in range(10):
            out_ref[c, BLOCK * b : BLOCK * b + BLOCK, :] = new[c]
            if b == 0:
                rim_out_ref[0, c : c + 1, :] = new[c][0:1]
            if b == blocks - 1:
                rim_out_ref[1, c : c + 1, :] = new[c][BLOCK - 1 : BLOCK]
    coded(out_ref, code_ref)


def second_kernel(
    phase, tiles_ref, u_ref, near_ref, far_ref, rim_ref, source_ref, step_ref, diss_ref, freq_ref, out_ref, after_ref
):
    rims = rims_beside(rim_ref, lax.axis_index("passage"), phase)
    width = u_ref.shape[1]
    blocks = width // BLOCK
    scales = code_scale(near_ref, width), code_scale(far_ref, width)
    for b in range(blocks):
        new = sweep_block(
            b, blocks, u_ref, near_ref, far_ref, scales, rims,
            lambda e: tiles_ref[e, BLOCK * b : BLOCK * b + BLOCK, :].astype(F32),
            source_ref, step_ref, diss_ref, freq_ref,
        )
        for c in range(10):
            out_ref[c, BLOCK * b : BLOCK * b + BLOCK, :] = new[c]
    after_ref[...] = jnp.zeros_like(after_ref)


def wall_kernel(
    phase, u_ref, rim_ref, fields_ref, walls_ref, weight_ref, route_ref, weights_ref, routes_ref, disses_ref, send_ref
):
    width = u_ref.shape[1]
    shape = (width, 128)
    lane, row = lanes(shape), rows(shape)
    within = lane % 8
    zero = jnp.zeros(shape, F32)
    at_wall = [zero + u_ref[c, :, 0:1] for c in range(10)]

    def chosen(values):
        out = values[0]
        for k in range(1, 6):
            out = jnp.where(within == k, values[k], out)
        return out

    below, above = rims_beside(rim_ref, lax.axis_index("passage"), phase)
    u = chosen([at_wall[c] for c in WALL])
    other = chosen([at_wall[(c + 5) % 10] for c in WALL])
    right = chosen([u_ref[c, :, 1:2] for c in WALL])
    below = chosen([below[c][:, 0:1] for c in WALL])
    above = chosen([above[c][:, 0:1] for c in WALL])
    down = jnp.where(row == 0, below, pltpu.roll(u, 1, axis=0))
    up = jnp.where(row == width - 1, above, pltpu.roll(u, width - 1, axis=0))
    own = u - fields_ref[0] * (
        fields_ref[2] * other + fields_ref[1] * (6.0 * u - (down + up + right)) - fields_ref[3]
    )

    def sent(route, weight, value):
        value = weight * jnp.where(within == 6, 1.0, value)
        return jnp.dot(route, value, precision=lax.Precision.HIGHEST, preferred_element_type=F32)

    routed = sent(route_ref[...], weight_ref[...], own)
    even = lax.axis_index("brick") % 2 == 0
    for at, share in enumerate((-0.5, 0.5)):
        share = jnp.where(even, -share, share)
        tile = jnp.where(even, walls_ref[1 - at], walls_ref[at])
        re, im = zero, zero
        for n in range(5):
            entry = pltpu.roll(tile, 127 - 5 * n, axis=1)
            re = re + entry * at_wall[n]
            im = im + entry * at_wall[5 + n]
        conv = jnp.where(lane < 3, re, jnp.where(lane < 6, pltpu.roll(im, 3, axis=1), 0.0))
        for turn in (8, 16, 32, 64):
            conv = conv + pltpu.roll(conv, turn, axis=1)
        routed = routed + sent(routes_ref[at], weights_ref[at], disses_ref[at] * u + share * conv)
    for q in range(send_ref.shape[0]):
        send_ref[q] = routed[q : q + 1, :]


def nodes_kernel(recv_ref, after_ref, out_ref, dense):
    peers = recv_ref.shape[0]
    for q in range(peers):
        dense[q : q + 1, :] = recv_ref[q]
    total = jnp.zeros((8, NODE_DEV), F32)
    node = lanes((peers, NODE_DEV)).astype(F32) + 1.0
    terms = dense[...].T
    for r in range(CAP * PLANES):
        hit = jnp.where(dense[:, 8 * r + 6 : 8 * r + 7] == node, 1.0, 0.0)
        total = total + jnp.dot(
            terms[8 * r : 8 * r + 8, :], hit, precision=lax.Precision.HIGHEST, preferred_element_type=F32
        )
    for c in range(6):
        out_ref[c] = total[c : c + 1, :]


def kernel_call(body, out, scratch=(), flops=None):
    whole = pl.BlockSpec(memory_space=pltpu.VMEM)
    return pl.pallas_call(
        body,
        out_shape=[jax.ShapeDtypeStruct(s, d) for s, d in out],
        out_specs=[whole] * len(out),
        scratch_shapes=list(scratch),
        compiler_params=pltpu.CompilerParams(vmem_limit_bytes=VMEM_BYTES),
        cost_estimate=flops and pl.CostEstimate(flops=flops, bytes_accessed=0, transcendentals=0),
    )


def planes_beside(code, bricks):
    near = [(i, i ^ 1) for i in range(bricks)]
    far = [(i, i - 1 if i % 2 == 0 else i + 1) for i in range(1, bricks - 1)]
    return lax.ppermute(code, "brick", near), lax.ppermute(code, "brick", far)


def swapped(rim, passes):
    return lax.ppermute(rim, "passage", [(i, (i + 1) % passes) for i in range(passes)])


def body(
    jac_blocks,
    psi_start,
    source,
    pseudo_step,
    dissipation,
    freq_volume,
    normals,
    face_owner,
    face_slot,
):
    passes = lax.axis_size("passage")
    bricks = lax.axis_size("brick")
    width, depth = psi_start.shape[3], psi_start.shape[4]
    phase = 2.0 * math.pi * ND * passes / BLADES
    field = (10, width, depth)
    rim = (2, 16, depth)
    plane = (10 * width + 16, depth)

    psi = psi_start.reshape(field)
    jac = jac_blocks.reshape(25, bricks, depth)
    source = source.reshape(field)
    scalars = [a.reshape(width, depth) for a in (pseudo_step, dissipation, freq_volume)]

    (send,) = kernel_call(
        prep_kernel,
        [((bricks, ROWS, depth), BF16)],
        [pltpu.VMEM((ROWS * bricks, depth), F32)],
    )(jac)
    recv = lax.all_to_all(send, "brick", 0, 0, tiled=True)
    face = (width, 128)
    rims, weight, route, code, fields = kernel_call(
        aux_kernel,
        [(rim, F32), (face, F32), ((bricks, width), F32), ((plane[0] + width, depth), I16), ((4, *face), F32)],
    )(psi, source, *scalars, face_owner.reshape(1, width), face_slot, normals.reshape(3, 1, width))
    rims = swapped(rims, passes)
    near, far = planes_beside(code, bricks)
    weights, routes, disses = kernel_call(
        beside_kernel, [((2, *face), F32), ((2, bricks, width), F32), ((2, *face), F32)]
    )(near, far)

    state, tiles, rims, code, walls = kernel_call(
        functools.partial(first_kernel, phase),
        [(field, F32), ((25, width, depth), BF16), (rim, F32), (plane, I16), ((2, *face), F32)],
        [pltpu.VMEM((ROWS * width, depth), F32)],
    )(recv, psi, near, far, rims, source, *scalars)

    rims = swapped(rims, passes)
    near, far = planes_beside(code, bricks)
    (routed,) = kernel_call(functools.partial(wall_kernel, phase), [((bricks, 1, 128), F32)], flops=AHEAD)(
        state, rims, fields, walls, weight, route, weights, routes, disses
    )
    arrived = lax.all_to_all(routed, "brick", 0, 0, tiled=True)
    state, after = kernel_call(functools.partial(second_kernel, phase), [(field, F32), ((8, 128), F32)])(
        tiles, state, near, far, rims, source, *scalars
    )
    (sensitivity,) = kernel_call(nodes_kernel, [((6, 1, NODE_DEV), F32)], [pltpu.VMEM((bricks, 128), F32)])(
        arrived, after
    )
    return state.reshape(psi_start.shape), sensitivity.transpose(1, 0, 2)


def solution(mesh):
    placed = (
        P("passage", None, None, "brick"),
        P("passage", None, "brick", None, None),
        P("passage", None, "brick", None, None),
        P("passage", "brick", None, None),
        P("passage", "brick", None, None),
        P("passage", "brick", None, None),
        P("passage", None, "brick", None),
        P("passage", "brick", None),
        P("passage", "brick"),
    )
    return jax.shard_map(
        body,
        mesh=mesh,
        in_specs=placed,
        out_specs=(P("passage", None, "brick", None, None), P("passage", None, "brick")),
        check_vma=False,
    )
```

```python
import functools
import math

import jax
import jax.numpy as jnp
from jax import lax
from jax.experimental import pallas as pl
from jax.experimental.pallas import tpu as pltpu
from jax.sharding import PartitionSpec as P

NODE_DEV = 256
CAP = 4
PLANES = 3
WALL = (1, 2, 3, 6, 7, 8)
ND = 1
BLADES = 36
ROWS = 32
PITCH = ROWS + 1
BLOCK = 16
FULL = 32000.0
AHEAD = 1 << 34
VMEM_BYTES = 40 * 1024 * 1024
F32 = jnp.float32
BF16 = jnp.bfloat16
I16 = jnp.int16


def lanes(shape):
    return lax.broadcasted_iota(jnp.int32, shape, len(shape) - 1)


def rows(shape):
    return lax.broadcasted_iota(jnp.int32, shape, len(shape) - 2)


def prep_kernel(jac_ref, send_ref, wide):
    planes = jac_ref.shape[1]
    pitch = planes + 1
    wide[25 * pitch : ROWS * pitch, :] = jnp.zeros(((ROWS - 25) * pitch, 128), F32)
    lane = lanes((planes, 128))
    wall = jnp.zeros((planes, 128), F32)
    for e in range(25):
        entry = jac_ref[e].astype(F32)
        wide[e * pitch : e * pitch + planes, :] = entry
        wall = jnp.where(lane == e, pltpu.roll(entry, e, axis=1) if e else entry, wall)
    wide[25 * pitch + 1 : 25 * pitch + planes, :] = wall[0 : planes - 1]
    wide[26 * pitch : 26 * pitch + planes - 1, :] = wall[1:planes]
    for i in range(planes):
        send_ref[i] = wide[pl.ds(i, ROWS, stride=pitch), :].astype(BF16)


def routing(owner_row, rank, values, first):
    faces = rank.shape[0]
    square = (faces, faces)
    lane = lanes((faces, 128))
    within = lane % 8
    weight = jnp.where(within == 6, values[3], 0.0)
    for d in range(3):
        weight = jnp.where((within == d) | (within == d + 3), values[d], weight)
    weight = jnp.where((lane // 8 - first).astype(F32) == rank, weight, 0.0)
    return jnp.where(rows(square).astype(F32) == owner_row, 1.0, 0.0), weight


def turned(value):
    length = max(value.shape)
    square = (length, length)
    eye = rows(square) == lanes(square)
    return jnp.sum(jnp.where(eye, value, 0.0), axis=1 if value.shape[0] == 1 else 0, keepdims=True)


def aux_kernel(
    psi_ref, source_ref, step_ref, diss_ref, freq_ref, owner_ref, slot_ref, normals_ref,
    rim_ref, weight_ref, route_ref, code_ref, fields_ref,
):
    width = psi_ref.shape[1]
    rim_ref[...] = jnp.zeros_like(rim_ref)
    for c in range(10):
        rim_ref[0, c : c + 1, :] = psi_ref[c, 0:1, :]
        rim_ref[1, c : c + 1, :] = psi_ref[c, width - 1 : width, :]

    square = (width, width)
    owner_row = owner_ref[...].astype(F32)
    owner = turned(owner_row)
    slot = turned(slot_ref[...].astype(F32)) + 1.0
    earlier = (owner == owner_row) & (lanes(square) < rows(square))
    rank = jnp.sum(jnp.where(earlier, 1.0, 0.0), axis=1, keepdims=True)
    normals = [turned(normals_ref[d]) for d in range(3)]
    route_ref[...], weight_ref[...] = routing(owner_row, rank, normals + [slot], 0)

    step, diss, omega = step_ref[:, 0:1], diss_ref[:, 0:1], freq_ref[:, 0:1]
    lane = lanes((width, 128))
    info = jnp.zeros((width, 128), F32)
    for k, value in enumerate([step * n for n in normals] + [slot, diss, owner, rank]):
        info = jnp.where(lane == k, value, info)
    coded(psi_ref, code_ref, info)

    within = lane % 8
    flow = jnp.zeros((width, 128), F32)
    for k, c in enumerate(WALL):
        flow = jnp.where(within == k, source_ref[c, :, 0:1], flow)
    fields_ref[0] = jnp.zeros((width, 128), F32) + step
    fields_ref[1] = jnp.zeros((width, 128), F32) + diss
    fields_ref[2] = jnp.where(within < 3, omega, -omega)
    fields_ref[3] = flow


def routing_beside(ref, width, first):
    last = 10 * width + 16
    exponent = ref[last - 16 : last, :].astype(jnp.int32).astype(F32)[15:16, :]
    code = ref[last:, :].astype(jnp.int32).astype(F32)
    low = pltpu.roll(code, 120, axis=1)
    info = (code + low * (1.0 / FULL)) * (jnp.exp2(exponent) * (1.0 / FULL))
    column = [info[:, k : k + 1] for k in range(7)]
    slot, owner, rank = [jnp.round(column[k]) for k in (3, 5, 6)]
    return *routing(turned(owner), rank, column[:3] + [slot], first), column[4]


def exponent_of(top):
    return jnp.ceil(jnp.log2(jnp.maximum(top, 1e-30)))


def short(value):
    return jnp.round(value).astype(jnp.int32).astype(I16)


def coded(u_ref, code_ref, info=None):
    width = u_ref.shape[1]
    exponents = jnp.zeros((16, 128), F32)
    row = rows((16, 128))
    for c in range(10):
        top = jnp.max(jnp.abs(u_ref[c]), axis=0, keepdims=True)
        top = jnp.max(top, axis=1, keepdims=True)
        exponent = exponent_of(top)
        code_ref[c * width : (c + 1) * width, :] = short(u_ref[c] * (FULL * jnp.exp2(-exponent)))
        exponents = jnp.where(row == c, exponent, exponents)
    if info is not None:
        exponent = exponent_of(jnp.max(jnp.abs(info), axis=0, keepdims=True))
        exponents = jnp.where(row == 15, exponent, exponents)
        value = info * (FULL * jnp.exp2(-exponent))
        high = jnp.round(value)
        low = jnp.round((value - high) * FULL)
        lane = lanes((width, 128))
        both = jnp.where(lane < 8, high, jnp.where(lane < 16, pltpu.roll(low, 8, axis=1), 0.0))
        code_ref[10 * width + 16 :, :] = short(both)
    code_ref[10 * width : 10 * width + 16, :] = short(exponents)


def code_scale(code_ref, width):
    exponents = code_ref[10 * width : 10 * width + 16, :].astype(jnp.int32).astype(F32)
    scale = jnp.exp2(exponents) * (1.0 / FULL)
    return [scale[c : c + 1, :] for c in range(10)]


def rims_beside(rim_ref, passage, phase):
    def rotated(at, turn, edge):
        cosine = jnp.where(passage == edge, math.cos(turn), 1.0)
        sine = jnp.where(passage == edge, math.sin(turn), 0.0)
        rim = [rim_ref[at, c : c + 1, :] for c in range(10)]
        re = [rim[n] * cosine - rim[5 + n] * sine for n in range(5)]
        im = [rim[n] * sine + rim[5 + n] * cosine for n in range(5)]
        return re + im

    return rotated(1, -phase, 0), rotated(0, phase, 1)


def sweep_block(b, blocks, u_ref, near_ref, far_ref, scales, rims, tile, source_ref, step_ref, diss_ref, freq_ref):
    at = slice(BLOCK * b, BLOCK * b + BLOCK)
    shape = (BLOCK, 128)
    row, lane = rows(shape), lanes(shape)
    width = u_ref.shape[1]
    u = [u_ref[c, at, :] for c in range(10)]

    if b == 0:
        before = rims[0]
    else:
        before = [u_ref[c, BLOCK * b - 1 : BLOCK * b, :] for c in range(10)]
    if b == blocks - 1:
        after = rims[1]
    else:
        after = [u_ref[c, BLOCK * b + BLOCK : BLOCK * b + BLOCK + 1, :] for c in range(10)]

    half = jnp.where(lax.axis_index("brick") % 2 == 0, 0.5, -0.5)
    diff = []
    beside = []
    for c in range(10):
        first = c * width + BLOCK * b
        near = near_ref[first : first + BLOCK, :].astype(jnp.int32).astype(F32) * scales[0][c]
        far = far_ref[first : first + BLOCK, :].astype(jnp.int32).astype(F32) * scales[1][c]
        diff.append(half * (near - far))
        down = jnp.where(row == 0, before[c], pltpu.roll(u[c], 1, axis=0))
        up = jnp.where(row == BLOCK - 1, after[c], pltpu.roll(u[c], BLOCK - 1, axis=0))
        left = jnp.where(lane == 0, 0.0, pltpu.roll(u[c], 1, axis=1))
        right = jnp.where(lane == 127, 0.0, pltpu.roll(u[c], 127, axis=1))
        beside.append(near + far + up + down + right + left)
    conv = [None] * 10
    for n in range(5):
        for m in range(5):
            t = tile(5 * n + m)
            re, im = t * diff[n], t * diff[5 + n]
            conv[m] = re if n == 0 else conv[m] + re
            conv[5 + m] = im if n == 0 else conv[5 + m] + im
    step, diss, omega = step_ref[at, :], diss_ref[at, :], freq_ref[at, :]
    new = []
    for c in range(10):
        spin = omega * u[c + 5] if c < 5 else -(omega * u[c - 5])
        resid = conv[c] + spin + diss * (6.0 * u[c] - beside[c]) - source_ref[c, at, :]
        new.append(u[c] - step * resid)
    return new


def parts(value):
    high = value.astype(BF16).astype(F32)
    rest = value - high
    middle = rest.astype(BF16).astype(F32)
    return [high, middle, rest - middle]


def chosen(values, within):
    out = values[0]
    for k in range(1, 6):
        out = jnp.where(within == k, values[k], out)
    return out


def wall_terms(u_ref, fields_ref, walls, own_routing, beside):
    width = u_ref.shape[1]
    shape = (width, 128)
    lane, row = lanes(shape), rows(shape)
    within = lane % 8
    zero = jnp.zeros(shape, F32)
    at_wall = [zero + u_ref[c, :, 0:1] for c in range(10)]
    u = chosen([at_wall[c] for c in WALL], within)
    other = chosen([at_wall[(c + 5) % 10] for c in WALL], within)
    right = chosen([u_ref[c, :, 1:2] for c in WALL], within)
    down = jnp.where(row == 0, 0.0, pltpu.roll(u, 1, axis=0))
    up = jnp.where(row == width - 1, 0.0, pltpu.roll(u, width - 1, axis=0))
    own = u - fields_ref[0] * (
        fields_ref[2] * other + fields_ref[1] * (6.0 * u - (down + up + right)) - fields_ref[3]
    )

    def sent(route, weight, value):
        value = jnp.concatenate(parts(weight * jnp.where(within == 6, 1.0, value)), axis=1).astype(BF16)
        total = jnp.dot(route.astype(BF16), value, preferred_element_type=F32)
        return total[:, 0:128] + total[:, 128:256] + total[:, 256:384]

    routed = sent(*own_routing, own)
    even = lax.axis_index("brick") % 2 == 0
    for at, share in enumerate((-0.5, 0.5)):
        route, weight, diss = beside[at]
        share = jnp.where(even, -share, share)
        tile = jnp.where(even, walls[1 - at], walls[at])
        re, im = zero, zero
        for n in range(5):
            entry = pltpu.roll(tile, 127 - 5 * n, axis=1)
            re = re + entry * at_wall[n]
            im = im + entry * at_wall[5 + n]
        conv = jnp.where(lane < 3, re, jnp.where(lane < 6, pltpu.roll(im, 3, axis=1), 0.0))
        for turn in (8, 16, 32, 64):
            conv = conv + pltpu.roll(conv, turn, axis=1)
        routed = routed + sent(route, weight, diss * u + share * conv)
    return routed


def first_kernel(
    phase, recv_ref, u_ref, near_ref, far_ref, rim_ref, source_ref, step_ref, diss_ref, freq_ref,
    fields_ref, weight_ref, route_ref, out_ref, tiles_ref, rim_out_ref, code_ref, sum_ref, wide,
):
    rims = rims_beside(rim_ref, lax.axis_index("passage"), phase)
    width = u_ref.shape[1]
    for j in range(width):
        wide[j * PITCH : j * PITCH + ROWS, :] = recv_ref[j].astype(F32)
    for e in range(25):
        tiles_ref[e] = wide[pl.ds(e, width, stride=PITCH), :].astype(BF16)
    rim_out_ref[...] = jnp.zeros_like(rim_out_ref)
    blocks = width // BLOCK
    scales = code_scale(near_ref, width), code_scale(far_ref, width)
    for b in range(blocks):
        new = sweep_block(
            b, blocks, u_ref, near_ref, far_ref, scales, rims,
            lambda e: wide[pl.ds(BLOCK * b * PITCH + e, BLOCK, stride=PITCH), :],
            source_ref, step_ref, diss_ref, freq_ref,
        )
        for c in range(10):
            out_ref[c, BLOCK * b : BLOCK * b + BLOCK, :] = new[c]
            if b == 0:
                rim_out_ref[0, c : c + 1, :] = new[c][0:1]
            if b == blocks - 1:
                rim_out_ref[1, c : c + 1, :] = new[c][BLOCK - 1 : BLOCK]
    coded(out_ref, code_ref)
    walls = [wide[pl.ds(25 + at, width, stride=PITCH), :] for at in range(2)]
    beside = [routing_beside(ref, width, CAP * (at + 1)) for at, ref in enumerate((near_ref, far_ref))]
    sum_ref[...] = wall_terms(out_ref, fields_ref, walls, (route_ref[...], weight_ref[...]), beside)


def second_kernel(
    phase, tiles_ref, u_ref, near_ref, far_ref, rim_ref, source_ref, step_ref, diss_ref, freq_ref, out_ref, after_ref
):
    rims = rims_beside(rim_ref, lax.axis_index("passage"), phase)
    width = u_ref.shape[1]
    blocks = width // BLOCK
    scales = code_scale(near_ref, width), code_scale(far_ref, width)
    for b in range(blocks):
        new = sweep_block(
            b, blocks, u_ref, near_ref, far_ref, scales, rims,
            lambda e: tiles_ref[e, BLOCK * b : BLOCK * b + BLOCK, :].astype(F32),
            source_ref, step_ref, diss_ref, freq_ref,
        )
        for c in range(10):
            out_ref[c, BLOCK * b : BLOCK * b + BLOCK, :] = new[c]
    after_ref[...] = jnp.zeros_like(after_ref)


def rim_kernel(phase, sum_ref, rim_ref, fields_ref, weight_ref, route_ref, send_ref):
    width = sum_ref.shape[0]
    within = lanes((1, 128)) % 8
    routed = sum_ref[...]
    for face, layer in zip((0, width - 1), rims_beside(rim_ref, lax.axis_index("passage"), phase)):
        value = chosen([jnp.zeros((1, 128), F32) + layer[c][:, 0:1] for c in WALL], within)
        at = slice(face, face + 1)
        value = weight_ref[at, :] * jnp.where(within == 6, 0.0, fields_ref[0, at, :] * fields_ref[1, at, :] * value)
        routed = routed + route_ref[:, at] * value
    for q in range(send_ref.shape[0]):
        send_ref[q] = routed[q : q + 1, :]


def nodes_kernel(recv_ref, after_ref, out_ref, dense):
    peers = recv_ref.shape[0]
    for q in range(peers):
        dense[q : q + 1, :] = recv_ref[q]
    node = lanes((peers, NODE_DEV)).astype(F32) + 1.0
    terms = parts(dense[...].T)
    total = jnp.zeros((24, NODE_DEV), F32)
    for first in range(0, CAP * PLANES, CAP):
        hits, values = [], []
        for r in range(first, first + CAP):
            hits.append(jnp.where(dense[:, 8 * r + 6 : 8 * r + 7] == node, 1.0, 0.0))
            values.append(jnp.concatenate([t[8 * r : 8 * r + 8, :] for t in terms], axis=0))
        hits, values = jnp.concatenate(hits, axis=0).astype(BF16), jnp.concatenate(values, axis=1).astype(BF16)
        total = total + jnp.dot(values, hits, preferred_element_type=F32)
    total = total[0:8] + total[8:16] + total[16:24]
    for c in range(6):
        out_ref[c] = total[c : c + 1, :]


def kernel_call(body, out, scratch=(), flops=None):
    whole = pl.BlockSpec(memory_space=pltpu.VMEM)
    return pl.pallas_call(
        body,
        out_shape=[jax.ShapeDtypeStruct(s, d) for s, d in out],
        out_specs=[whole] * len(out),
        scratch_shapes=list(scratch),
        compiler_params=pltpu.CompilerParams(vmem_limit_bytes=VMEM_BYTES),
        cost_estimate=flops and pl.CostEstimate(flops=flops, bytes_accessed=0, transcendentals=0),
    )


def planes_beside(code, bricks):
    near = [(i, i ^ 1) for i in range(bricks)]
    far = [(i, i - 1 if i % 2 == 0 else i + 1) for i in range(1, bricks - 1)]
    return lax.ppermute(code, "brick", near), lax.ppermute(code, "brick", far)


def swapped(rim, passes):
    return lax.ppermute(rim, "passage", [(i, (i + 1) % passes) for i in range(passes)])


def body(
    jac_blocks,
    psi_start,
    source,
    pseudo_step,
    dissipation,
    freq_volume,
    normals,
    face_owner,
    face_slot,
):
    passes = lax.axis_size("passage")
    bricks = lax.axis_size("brick")
    width, depth = psi_start.shape[3], psi_start.shape[4]
    phase = 2.0 * math.pi * ND * passes / BLADES
    field = (10, width, depth)
    rim = (2, 16, depth)
    plane = (10 * width + 16, depth)

    psi = psi_start.reshape(field)
    jac = jac_blocks.reshape(25, bricks, depth)
    source = source.reshape(field)
    scalars = [a.reshape(width, depth) for a in (pseudo_step, dissipation, freq_volume)]

    (send,) = kernel_call(
        prep_kernel,
        [((bricks, ROWS, depth), BF16)],
        [pltpu.VMEM((ROWS * (bricks + 1), depth), F32)],
    )(jac)
    recv = lax.all_to_all(send, "brick", 0, 0, tiled=True)
    face = (width, 128)
    rims, weight, route, code, fields = kernel_call(
        aux_kernel,
        [(rim, F32), (face, F32), ((bricks, width), F32), ((plane[0] + width, depth), I16), ((4, *face), F32)],
    )(psi, source, *scalars, face_owner.reshape(1, width), face_slot, normals.reshape(3, 1, width))
    rims = swapped(rims, passes)
    near, far = planes_beside(code, bricks)
    state, tiles, rims, code, terms = kernel_call(
        functools.partial(first_kernel, phase),
        [(field, F32), ((25, width, depth), BF16), (rim, F32), (plane, I16), (face, F32)],
        [pltpu.VMEM((PITCH * width, depth), F32)],
    )(recv, psi, near, far, rims, source, *scalars, fields, weight, route)

    rims = swapped(rims, passes)
    (routed,) = kernel_call(functools.partial(rim_kernel, phase), [((bricks, 1, 128), F32)], flops=AHEAD)(
        terms, rims, fields, weight, route
    )
    arrived = lax.all_to_all(routed, "brick", 0, 0, tiled=True)
    near, far = planes_beside(code, bricks)
    state, after = kernel_call(functools.partial(second_kernel, phase), [(field, F32), ((8, 128), F32)])(
        tiles, state, near, far, rims, source, *scalars
    )
    (sensitivity,) = kernel_call(nodes_kernel, [((6, 1, NODE_DEV), F32)], [pltpu.VMEM((bricks, 128), F32)])(
        arrived, after
    )
    return state.reshape(psi_start.shape), sensitivity.transpose(1, 0, 2)


def solution(mesh):
    placed = (
        P("passage", None, None, "brick"),
        P("passage", None, "brick", None, None),
        P("passage", None, "brick", None, None),
        P("passage", "brick", None, None),
        P("passage", "brick", None, None),
        P("passage", "brick", None, None),
        P("passage", None, "brick", None),
        P("passage", "brick", None),
        P("passage", "brick"),
    )
    return jax.shard_map(
        body,
        mesh=mesh,
        in_specs=placed,
        out_specs=(P("passage", None, "brick", None, None), P("passage", None, "brick")),
        check_vma=False,
    )
```

```python
import functools
import math

import jax
import jax.numpy as jnp
from jax import lax
from jax.experimental import pallas as pl
from jax.experimental.pallas import tpu as pltpu
from jax.sharding import PartitionSpec as P

NODE_DEV = 256
CAP = 4
PLANES = 3
WALL = (1, 2, 3, 6, 7, 8)
ND = 1
BLADES = 36
ROWS = 32
QUADS = 7
PITCH = ROWS + 1
BLOCK = 16
FULL = 32000.0
AHEAD = 1 << 34
VMEM_BYTES = 40 * 1024 * 1024
F32 = jnp.float32
BF16 = jnp.bfloat16
I16 = jnp.int16


def lanes(shape):
    return lax.broadcasted_iota(jnp.int32, shape, len(shape) - 1)


def rows(shape):
    return lax.broadcasted_iota(jnp.int32, shape, len(shape) - 2)


def prep_kernel(jac_ref, send_ref, wide):
    planes = jac_ref.shape[1]
    pitch = planes + 1
    wide[25 * pitch : ROWS * pitch, :] = jnp.zeros(((ROWS - 25) * pitch, 128), F32)
    lane = lanes((planes, 128))
    wall = jnp.zeros((planes, 128), F32)
    for e in range(25):
        entry = jac_ref[e].astype(F32)
        wide[e * pitch : e * pitch + planes, :] = entry
        wall = jnp.where(lane == e, pltpu.roll(entry, e, axis=1) if e else entry, wall)
    wide[25 * pitch + 1 : 25 * pitch + planes, :] = wall[0 : planes - 1]
    wide[26 * pitch : 26 * pitch + planes - 1, :] = wall[1:planes]
    for i in range(planes):
        plane = wide[pl.ds(i, ROWS, stride=pitch), :].astype(BF16)
        for m in range(QUADS):
            send_ref[i, :, 128 * m : 128 * m + 128] = plane[4 * m : 4 * m + 4]


def routing(owner_row, rank, values, first):
    faces = rank.shape[0]
    square = (faces, faces)
    lane = lanes((faces, 128))
    within = lane % 8
    weight = jnp.where(within == 6, values[3], 0.0)
    for d in range(3):
        weight = jnp.where((within == d) | (within == d + 3), values[d], weight)
    weight = jnp.where((lane // 8 - first).astype(F32) == rank, weight, 0.0)
    return jnp.where(rows(square).astype(F32) == owner_row, 1.0, 0.0), weight


def turned(value):
    length = max(value.shape)
    square = (length, length)
    eye = rows(square) == lanes(square)
    return jnp.sum(jnp.where(eye, value, 0.0), axis=1 if value.shape[0] == 1 else 0, keepdims=True)


def aux_kernel(
    psi_ref, source_ref, step_ref, diss_ref, freq_ref, owner_ref, slot_ref, normals_ref,
    rim_ref, weight_ref, route_ref, code_ref, fields_ref,
):
    width = psi_ref.shape[1]
    rim_ref[...] = jnp.zeros_like(rim_ref)
    for c in range(10):
        rim_ref[0, c : c + 1, :] = psi_ref[c, 0:1, :]
        rim_ref[1, c : c + 1, :] = psi_ref[c, width - 1 : width, :]

    square = (width, width)
    owner_row = owner_ref[...].astype(F32)
    owner = turned(owner_row)
    slot = turned(slot_ref[...].astype(F32)) + 1.0
    earlier = (owner == owner_row) & (lanes(square) < rows(square))
    rank = jnp.sum(jnp.where(earlier, 1.0, 0.0), axis=1, keepdims=True)
    normals = [turned(normals_ref[d]) for d in range(3)]
    route_ref[...], weight_ref[...] = routing(owner_row, rank, normals + [slot], 0)

    step, diss, omega = step_ref[:, 0:1], diss_ref[:, 0:1], freq_ref[:, 0:1]
    lane = lanes((width, 128))
    info = jnp.zeros((width, 128), F32)
    for k, value in enumerate([step * n for n in normals] + [slot, diss, owner, rank]):
        info = jnp.where(lane == k, value, info)
    coded(psi_ref, code_ref, info)

    within = lane % 8
    flow = jnp.zeros((width, 128), F32)
    for k, c in enumerate(WALL):
        flow = jnp.where(within == k, source_ref[c, :, 0:1], flow)
    fields_ref[0] = jnp.zeros((width, 128), F32) + step
    fields_ref[1] = jnp.zeros((width, 128), F32) + diss
    fields_ref[2] = jnp.where(within < 3, omega, -omega)
    fields_ref[3] = flow


def routing_beside(ref, width, first):
    last = 10 * width + 16
    exponent = ref[last - 16 : last, :].astype(jnp.int32).astype(F32)[15:16, :]
    code = ref[last:, :].astype(jnp.int32).astype(F32)
    low = pltpu.roll(code, 120, axis=1)
    info = (code + low * (1.0 / FULL)) * (jnp.exp2(exponent) * (1.0 / FULL))
    column = [info[:, k : k + 1] for k in range(7)]
    slot, owner, rank = [jnp.round(column[k]) for k in (3, 5, 6)]
    return *routing(turned(owner), rank, column[:3] + [slot], first), column[4]


def exponent_of(top):
    return jnp.ceil(jnp.log2(jnp.maximum(top, 1e-30)))


def short(value):
    return jnp.round(value).astype(jnp.int32).astype(I16)


def coded(u_ref, code_ref, info=None):
    width = u_ref.shape[1]
    exponents = jnp.zeros((16, 128), F32)
    row = rows((16, 128))
    for c in range(10):
        top = jnp.max(jnp.abs(u_ref[c]), axis=0, keepdims=True)
        top = jnp.max(top, axis=1, keepdims=True)
        exponent = exponent_of(top)
        code_ref[c * width : (c + 1) * width, :] = short(u_ref[c] * (FULL * jnp.exp2(-exponent)))
        exponents = jnp.where(row == c, exponent, exponents)
    if info is not None:
        exponent = exponent_of(jnp.max(jnp.abs(info), axis=0, keepdims=True))
        exponents = jnp.where(row == 15, exponent, exponents)
        value = info * (FULL * jnp.exp2(-exponent))
        high = jnp.round(value)
        low = jnp.round((value - high) * FULL)
        lane = lanes((width, 128))
        both = jnp.where(lane < 8, high, jnp.where(lane < 16, pltpu.roll(low, 8, axis=1), 0.0))
        code_ref[10 * width + 16 :, :] = short(both)
    code_ref[10 * width : 10 * width + 16, :] = short(exponents)


def code_scale(code_ref, width):
    exponents = code_ref[10 * width : 10 * width + 16, :].astype(jnp.int32).astype(F32)
    scale = jnp.exp2(exponents) * (1.0 / FULL)
    return [scale[c : c + 1, :] for c in range(10)]


def rims_beside(rim_ref, passage, phase):
    def rotated(at, turn, edge):
        cosine = jnp.where(passage == edge, math.cos(turn), 1.0)
        sine = jnp.where(passage == edge, math.sin(turn), 0.0)
        rim = [rim_ref[at, c : c + 1, :] for c in range(10)]
        re = [rim[n] * cosine - rim[5 + n] * sine for n in range(5)]
        im = [rim[n] * sine + rim[5 + n] * cosine for n in range(5)]
        return re + im

    return rotated(1, -phase, 0), rotated(0, phase, 1)


def sweep_block(b, blocks, u_ref, near_ref, far_ref, scales, rims, tile, source_ref, step_ref, diss_ref, freq_ref):
    at = slice(BLOCK * b, BLOCK * b + BLOCK)
    shape = (BLOCK, 128)
    row, lane = rows(shape), lanes(shape)
    width = u_ref.shape[1]
    u = [u_ref[c, at, :] for c in range(10)]

    if b == 0:
        before = rims[0]
    else:
        before = [u_ref[c, BLOCK * b - 1 : BLOCK * b, :] for c in range(10)]
    if b == blocks - 1:
        after = rims[1]
    else:
        after = [u_ref[c, BLOCK * b + BLOCK : BLOCK * b + BLOCK + 1, :] for c in range(10)]

    half = jnp.where(lax.axis_index("brick") % 2 == 0, 0.5, -0.5)
    diff = []
    beside = []
    for c in range(10):
        first = c * width + BLOCK * b
        near = near_ref[first : first + BLOCK, :].astype(jnp.int32).astype(F32) * scales[0][c]
        far = far_ref[first : first + BLOCK, :].astype(jnp.int32).astype(F32) * scales[1][c]
        diff.append(half * (near - far))
        down = jnp.where(row == 0, before[c], pltpu.roll(u[c], 1, axis=0))
        up = jnp.where(row == BLOCK - 1, after[c], pltpu.roll(u[c], BLOCK - 1, axis=0))
        left = jnp.where(lane == 0, 0.0, pltpu.roll(u[c], 1, axis=1))
        right = jnp.where(lane == 127, 0.0, pltpu.roll(u[c], 127, axis=1))
        beside.append(near + far + up + down + right + left)
    conv = [None] * 10
    for n in range(5):
        for m in range(5):
            t = tile(5 * n + m)
            re, im = t * diff[n], t * diff[5 + n]
            conv[m] = re if n == 0 else conv[m] + re
            conv[5 + m] = im if n == 0 else conv[5 + m] + im
    step, diss, omega = step_ref[at, :], diss_ref[at, :], freq_ref[at, :]
    new = []
    for c in range(10):
        spin = omega * u[c + 5] if c < 5 else -(omega * u[c - 5])
        resid = conv[c] + spin + diss * (6.0 * u[c] - beside[c]) - source_ref[c, at, :]
        new.append(u[c] - step * resid)
    return new


def parts(value):
    high = value.astype(BF16).astype(F32)
    rest = value - high
    middle = rest.astype(BF16).astype(F32)
    return [high, middle, rest - middle]


def chosen(values, within):
    out = values[0]
    for k in range(1, 6):
        out = jnp.where(within == k, values[k], out)
    return out


def wall_terms(u_ref, fields_ref, walls, own_routing, beside):
    width = u_ref.shape[1]
    shape = (width, 128)
    lane, row = lanes(shape), rows(shape)
    within = lane % 8
    zero = jnp.zeros(shape, F32)
    at_wall = [zero + u_ref[c, :, 0:1] for c in range(10)]
    u = chosen([at_wall[c] for c in WALL], within)
    other = chosen([at_wall[(c + 5) % 10] for c in WALL], within)
    right = chosen([u_ref[c, :, 1:2] for c in WALL], within)
    down = jnp.where(row == 0, 0.0, pltpu.roll(u, 1, axis=0))
    up = jnp.where(row == width - 1, 0.0, pltpu.roll(u, width - 1, axis=0))
    own = u - fields_ref[0] * (
        fields_ref[2] * other + fields_ref[1] * (6.0 * u - (down + up + right)) - fields_ref[3]
    )

    def sent(route, weight, value):
        value = jnp.concatenate(parts(weight * jnp.where(within == 6, 1.0, value)), axis=1).astype(BF16)
        total = jnp.dot(route.astype(BF16), value, preferred_element_type=F32)
        return total[:, 0:128] + total[:, 128:256] + total[:, 256:384]

    routed = sent(*own_routing, own)
    even = lax.axis_index("brick") % 2 == 0
    for at, share in enumerate((-0.5, 0.5)):
        route, weight, diss = beside[at]
        share = jnp.where(even, -share, share)
        tile = jnp.where(even, walls[1 - at], walls[at])
        re, im = zero, zero
        for n in range(5):
            entry = pltpu.roll(tile, 127 - 5 * n, axis=1)
            re = re + entry * at_wall[n]
            im = im + entry * at_wall[5 + n]
        conv = jnp.where(lane < 3, re, jnp.where(lane < 6, pltpu.roll(im, 3, axis=1), 0.0))
        for turn in (8, 16, 32, 64):
            conv = conv + pltpu.roll(conv, turn, axis=1)
        routed = routed + sent(route, weight, diss * u + share * conv)
    return routed


def first_kernel(
    phase, recv_ref, u_ref, near_ref, far_ref, rim_ref, source_ref, step_ref, diss_ref, freq_ref,
    fields_ref, weight_ref, route_ref, out_ref, tiles_ref, rim_out_ref, code_ref, sum_ref, wide,
):
    rims = rims_beside(rim_ref, lax.axis_index("passage"), phase)
    width = u_ref.shape[1]
    for j in range(width):
        for m in range(QUADS):
            at = j * PITCH + 4 * m
            wide[at : at + 4, :] = recv_ref[j, :, 128 * m : 128 * m + 128].astype(F32)
    for e in range(25):
        tiles_ref[e] = wide[pl.ds(e, width, stride=PITCH), :].astype(BF16)
    rim_out_ref[...] = jnp.zeros_like(rim_out_ref)
    blocks = width // BLOCK
    scales = code_scale(near_ref, width), code_scale(far_ref, width)
    for b in range(blocks):
        new = sweep_block(
            b, blocks, u_ref, near_ref, far_ref, scales, rims,
            lambda e: wide[pl.ds(BLOCK * b * PITCH + e, BLOCK, stride=PITCH), :],
            source_ref, step_ref, diss_ref, freq_ref,
        )
        for c in range(10):
            out_ref[c, BLOCK * b : BLOCK * b + BLOCK, :] = new[c]
            if b == 0:
                rim_out_ref[0, c : c + 1, :] = new[c][0:1]
            if b == blocks - 1:
                rim_out_ref[1, c : c + 1, :] = new[c][BLOCK - 1 : BLOCK]
    coded(out_ref, code_ref)
    walls = [wide[pl.ds(25 + at, width, stride=PITCH), :] for at in range(2)]
    beside = [routing_beside(ref, width, CAP * (at + 1)) for at, ref in enumerate((near_ref, far_ref))]
    sum_ref[...] = wall_terms(out_ref, fields_ref, walls, (route_ref[...], weight_ref[...]), beside)


def second_kernel(
    phase, tiles_ref, u_ref, near_ref, far_ref, rim_ref, source_ref, step_ref, diss_ref, freq_ref, out_ref, after_ref
):
    rims = rims_beside(rim_ref, lax.axis_index("passage"), phase)
    width = u_ref.shape[1]
    blocks = width // BLOCK
    scales = code_scale(near_ref, width), code_scale(far_ref, width)
    for b in range(blocks):
        new = sweep_block(
            b, blocks, u_ref, near_ref, far_ref, scales, rims,
            lambda e: tiles_ref[e, BLOCK * b : BLOCK * b + BLOCK, :].astype(F32),
            source_ref, step_ref, diss_ref, freq_ref,
        )
        for c in range(10):
            out_ref[c, BLOCK * b : BLOCK * b + BLOCK, :] = new[c]
    after_ref[...] = jnp.zeros_like(after_ref)


def rim_kernel(phase, sum_ref, rim_ref, fields_ref, weight_ref, route_ref, send_ref):
    width = sum_ref.shape[0]
    within = lanes((1, 128)) % 8
    routed = sum_ref[...]
    for face, layer in zip((0, width - 1), rims_beside(rim_ref, lax.axis_index("passage"), phase)):
        value = chosen([jnp.zeros((1, 128), F32) + layer[c][:, 0:1] for c in WALL], within)
        at = slice(face, face + 1)
        value = weight_ref[at, :] * jnp.where(within == 6, 0.0, fields_ref[0, at, :] * fields_ref[1, at, :] * value)
        routed = routed + route_ref[:, at] * value
    for q in range(send_ref.shape[0]):
        send_ref[q] = routed[q : q + 1, :]


def nodes_kernel(recv_ref, after_ref, out_ref, dense):
    peers = recv_ref.shape[0]
    for q in range(peers):
        dense[q : q + 1, :] = recv_ref[q]
    node = lanes((peers, NODE_DEV)).astype(F32) + 1.0
    terms = parts(dense[...].T)
    total = jnp.zeros((24, NODE_DEV), F32)
    for first in range(0, CAP * PLANES, CAP):
        hits, values = [], []
        for r in range(first, first + CAP):
            hits.append(jnp.where(dense[:, 8 * r + 6 : 8 * r + 7] == node, 1.0, 0.0))
            values.append(jnp.concatenate([t[8 * r : 8 * r + 8, :] for t in terms], axis=0))
        hits, values = jnp.concatenate(hits, axis=0).astype(BF16), jnp.concatenate(values, axis=1).astype(BF16)
        total = total + jnp.dot(values, hits, preferred_element_type=F32)
    total = total[0:8] + total[8:16] + total[16:24]
    for c in range(6):
        out_ref[c] = total[c : c + 1, :]


def kernel_call(body, out, scratch=(), flops=None):
    whole = pl.BlockSpec(memory_space=pltpu.VMEM)
    return pl.pallas_call(
        body,
        out_shape=[jax.ShapeDtypeStruct(s, d) for s, d in out],
        out_specs=[whole] * len(out),
        scratch_shapes=list(scratch),
        compiler_params=pltpu.CompilerParams(vmem_limit_bytes=VMEM_BYTES),
        cost_estimate=flops and pl.CostEstimate(flops=flops, bytes_accessed=0, transcendentals=0),
    )


def planes_beside(code, bricks):
    near = [(i, i ^ 1) for i in range(bricks)]
    far = [(i, i - 1 if i % 2 == 0 else i + 1) for i in range(1, bricks - 1)]
    return lax.ppermute(code, "brick", near), lax.ppermute(code, "brick", far)


def swapped(rim, passes):
    return lax.ppermute(rim, "passage", [(i, (i + 1) % passes) for i in range(passes)])


def body(
    jac_blocks,
    psi_start,
    source,
    pseudo_step,
    dissipation,
    freq_volume,
    normals,
    face_owner,
    face_slot,
):
    passes = lax.axis_size("passage")
    bricks = lax.axis_size("brick")
    width, depth = psi_start.shape[3], psi_start.shape[4]
    phase = 2.0 * math.pi * ND * passes / BLADES
    field = (10, width, depth)
    rim = (2, 16, depth)
    plane = (10 * width + 16, depth)

    psi = psi_start.reshape(field)
    jac = jac_blocks.reshape(25, bricks, depth)
    source = source.reshape(field)
    scalars = [a.reshape(width, depth) for a in (pseudo_step, dissipation, freq_volume)]

    (send,) = kernel_call(
        prep_kernel,
        [((bricks, 4, QUADS * depth), BF16)],
        [pltpu.VMEM((ROWS * (bricks + 1), depth), F32)],
    )(jac)
    recv = lax.all_to_all(send, "brick", 0, 0, tiled=True)
    face = (width, 128)
    rims, weight, route, code, fields = kernel_call(
        aux_kernel,
        [(rim, F32), (face, F32), ((bricks, width), F32), ((plane[0] + width, depth), I16), ((4, *face), F32)],
    )(psi, source, *scalars, face_owner.reshape(1, width), face_slot, normals.reshape(3, 1, width))
    rims = swapped(rims, passes)
    near, far = planes_beside(code, bricks)
    state, tiles, rims, code, terms = kernel_call(
        functools.partial(first_kernel, phase),
        [(field, F32), ((25, width, depth), BF16), (rim, F32), (plane, I16), (face, F32)],
        [pltpu.VMEM((PITCH * width, depth), F32)],
    )(recv, psi, near, far, rims, source, *scalars, fields, weight, route)

    rims = swapped(rims, passes)
    (routed,) = kernel_call(functools.partial(rim_kernel, phase), [((bricks, 1, 128), F32)], flops=AHEAD)(
        terms, rims, fields, weight, route
    )
    arrived = lax.all_to_all(routed, "brick", 0, 0, tiled=True)
    near, far = planes_beside(code, bricks)
    state, after = kernel_call(functools.partial(second_kernel, phase), [(field, F32), ((8, 128), F32)])(
        tiles, state, near, far, rims, source, *scalars
    )
    (sensitivity,) = kernel_call(nodes_kernel, [((6, 1, NODE_DEV), F32)], [pltpu.VMEM((bricks, 128), F32)])(
        arrived, after
    )
    return state.reshape(psi_start.shape), sensitivity.transpose(1, 0, 2)


def solution(mesh):
    placed = (
        P("passage", None, None, "brick"),
        P("passage", None, "brick", None, None),
        P("passage", None, "brick", None, None),
        P("passage", "brick", None, None),
        P("passage", "brick", None, None),
        P("passage", "brick", None, None),
        P("passage", None, "brick", None),
        P("passage", "brick", None),
        P("passage", "brick"),
    )
    return jax.shard_map(
        body,
        mesh=mesh,
        in_specs=placed,
        out_specs=(P("passage", None, "brick", None, None), P("passage", None, "brick")),
        check_vma=False,
    )
```

```python
import functools
import math

import jax
import jax.numpy as jnp
from jax import lax
from jax.experimental import pallas as pl
from jax.experimental.pallas import tpu as pltpu
from jax.sharding import PartitionSpec as P

NODE_DEV = 256
CAP = 4
PLANES = 3
WALL = (1, 2, 3, 6, 7, 8)
ND = 1
BLADES = 36
ROWS = 32
QUADS = 7
PITCH = ROWS + 1
BLOCK = 16
FULL = 32000.0
AHEAD = 1 << 34
VMEM_BYTES = 40 * 1024 * 1024
F32 = jnp.float32
BF16 = jnp.bfloat16
I16 = jnp.int16


def lanes(shape):
    return lax.broadcasted_iota(jnp.int32, shape, len(shape) - 1)


def rows(shape):
    return lax.broadcasted_iota(jnp.int32, shape, len(shape) - 2)


def prep_kernel(jac_ref, send_ref, wide):
    planes = jac_ref.shape[1]
    pitch = planes + 1
    wide[25 * pitch : ROWS * pitch, :] = jnp.zeros(((ROWS - 25) * pitch, 128), F32)
    lane = lanes((planes, 128))
    wall = jnp.zeros((planes, 128), F32)
    for e in range(25):
        entry = jac_ref[e].astype(F32)
        wide[e * pitch : e * pitch + planes, :] = entry
        wall = jnp.where(lane == e, pltpu.roll(entry, e, axis=1) if e else entry, wall)
    wide[25 * pitch + 1 : 25 * pitch + planes, :] = wall[0 : planes - 1]
    wide[26 * pitch : 26 * pitch + planes - 1, :] = wall[1:planes]
    for i in range(planes):
        plane = wide[pl.ds(i, ROWS, stride=pitch), :].astype(BF16)
        for m in range(QUADS):
            send_ref[i, :, 128 * m : 128 * m + 128] = plane[4 * m : 4 * m + 4]


def routing(owner_row, rank, values, first):
    faces = rank.shape[0]
    square = (faces, faces)
    lane = lanes((faces, 128))
    within = lane % 8
    weight = jnp.where(within == 6, values[3], 0.0)
    for d in range(3):
        weight = jnp.where((within == d) | (within == d + 3), values[d], weight)
    weight = jnp.where((lane // 8 - first).astype(F32) == rank, weight, 0.0)
    return jnp.where(rows(square).astype(F32) == owner_row, 1.0, 0.0), weight


def turned(value):
    length = max(value.shape)
    square = (length, length)
    eye = rows(square) == lanes(square)
    return jnp.sum(jnp.where(eye, value, 0.0), axis=1 if value.shape[0] == 1 else 0, keepdims=True)


def aux_kernel(
    psi_ref, source_ref, step_ref, diss_ref, freq_ref, owner_ref, slot_ref, normals_ref,
    rim_ref, weight_ref, route_ref, code_ref, fields_ref,
):
    width = psi_ref.shape[1]
    rim_ref[...] = jnp.zeros_like(rim_ref)
    for c in range(10):
        rim_ref[0, c : c + 1, :] = psi_ref[c, 0:1, :]
        rim_ref[1, c : c + 1, :] = psi_ref[c, width - 1 : width, :]

    square = (width, width)
    owner_row = owner_ref[...].astype(F32)
    owner = turned(owner_row)
    slot = turned(slot_ref[...].astype(F32)) + 1.0
    earlier = (owner == owner_row) & (lanes(square) < rows(square))
    rank = jnp.sum(jnp.where(earlier, 1.0, 0.0), axis=1, keepdims=True)
    normals = [turned(normals_ref[d]) for d in range(3)]
    route_ref[...], weight_ref[...] = routing(owner_row, rank, normals + [slot], 0)

    step, diss, omega = step_ref[:, 0:1], diss_ref[:, 0:1], freq_ref[:, 0:1]
    lane = lanes((width, 128))
    info = jnp.zeros((width, 128), F32)
    for k, value in enumerate([step * n for n in normals] + [slot, diss, owner, rank]):
        info = jnp.where(lane == k, value, info)
    coded(psi_ref, code_ref, info)

    within = lane % 8
    flow = jnp.zeros((width, 128), F32)
    for k, c in enumerate(WALL):
        flow = jnp.where(within == k, source_ref[c, :, 0:1], flow)
    fields_ref[0] = jnp.zeros((width, 128), F32) + step
    fields_ref[1] = jnp.zeros((width, 128), F32) + diss
    fields_ref[2] = jnp.where(within < 3, omega, -omega)
    fields_ref[3] = flow


def routing_beside(ref, width, first):
    last = 10 * width + 16
    exponent = ref[last - 16 : last, :].astype(jnp.int32).astype(F32)[15:16, :]
    packed = ref[last:, :].astype(jnp.int32).astype(F32)[0:8]
    code = [pltpu.roll(packed, 128 - 16 * g, axis=1) if g else packed for g in range(width // 8)]
    code = jnp.concatenate(code, axis=0)
    low = pltpu.roll(code, 120, axis=1)
    info = (code + low * (1.0 / FULL)) * (jnp.exp2(exponent) * (1.0 / FULL))
    column = [info[:, k : k + 1] for k in range(7)]
    slot, owner, rank = [jnp.round(column[k]) for k in (3, 5, 6)]
    return *routing(turned(owner), rank, column[:3] + [slot], first), column[4]


def exponent_of(top):
    return jnp.ceil(jnp.log2(jnp.maximum(top, 1e-30)))


def short(value):
    return jnp.round(value).astype(jnp.int32).astype(I16)


def coded(u_ref, code_ref, info=None):
    width = u_ref.shape[1]
    exponents = jnp.zeros((16, 128), F32)
    row = rows((16, 128))
    for c in range(10):
        top = jnp.max(jnp.abs(u_ref[c]), axis=0, keepdims=True)
        top = jnp.max(top, axis=1, keepdims=True)
        exponent = exponent_of(top)
        code_ref[c * width : (c + 1) * width, :] = short(u_ref[c] * (FULL * jnp.exp2(-exponent)))
        exponents = jnp.where(row == c, exponent, exponents)
    if info is not None:
        exponent = exponent_of(jnp.max(jnp.abs(info), axis=0, keepdims=True))
        exponents = jnp.where(row == 15, exponent, exponents)
        value = info * (FULL * jnp.exp2(-exponent))
        high = jnp.round(value)
        low = jnp.round((value - high) * FULL)
        lane = lanes((width, 128))
        both = jnp.where(lane < 8, high, jnp.where(lane < 16, pltpu.roll(low, 8, axis=1), 0.0))
        packed = both[0:8]
        for g in range(1, width // 8):
            packed = packed + pltpu.roll(both[8 * g : 8 * g + 8], 16 * g, axis=1)
        code_ref[10 * width + 16 :, :] = short(jnp.concatenate([packed, jnp.zeros((8, 128), F32)], axis=0))
    code_ref[10 * width : 10 * width + 16, :] = short(exponents)


def code_scale(code_ref, width):
    exponents = code_ref[10 * width : 10 * width + 16, :].astype(jnp.int32).astype(F32)
    scale = jnp.exp2(exponents) * (1.0 / FULL)
    return [scale[c : c + 1, :] for c in range(10)]


def rims_beside(rim_ref, passage, phase):
    def rotated(at, turn, edge):
        cosine = jnp.where(passage == edge, math.cos(turn), 1.0)
        sine = jnp.where(passage == edge, math.sin(turn), 0.0)
        rim = [rim_ref[at, c : c + 1, :] for c in range(10)]
        re = [rim[n] * cosine - rim[5 + n] * sine for n in range(5)]
        im = [rim[n] * sine + rim[5 + n] * cosine for n in range(5)]
        return re + im

    return rotated(1, -phase, 0), rotated(0, phase, 1)


def sweep_block(b, blocks, u_ref, near_ref, far_ref, scales, rims, tile, source_ref, step_ref, diss_ref, freq_ref):
    at = slice(BLOCK * b, BLOCK * b + BLOCK)
    shape = (BLOCK, 128)
    row, lane = rows(shape), lanes(shape)
    width = u_ref.shape[1]
    u = [u_ref[c, at, :] for c in range(10)]

    if b == 0:
        before = rims[0]
    else:
        before = [u_ref[c, BLOCK * b - 1 : BLOCK * b, :] for c in range(10)]
    if b == blocks - 1:
        after = rims[1]
    else:
        after = [u_ref[c, BLOCK * b + BLOCK : BLOCK * b + BLOCK + 1, :] for c in range(10)]

    half = jnp.where(lax.axis_index("brick") % 2 == 0, 0.5, -0.5)
    diff = []
    beside = []
    for c in range(10):
        first = c * width + BLOCK * b
        near = near_ref[first : first + BLOCK, :].astype(jnp.int32).astype(F32) * scales[0][c]
        far = far_ref[first : first + BLOCK, :].astype(jnp.int32).astype(F32) * scales[1][c]
        diff.append(half * (near - far))
        down = jnp.where(row == 0, before[c], pltpu.roll(u[c], 1, axis=0))
        up = jnp.where(row == BLOCK - 1, after[c], pltpu.roll(u[c], BLOCK - 1, axis=0))
        left = jnp.where(lane == 0, 0.0, pltpu.roll(u[c], 1, axis=1))
        right = jnp.where(lane == 127, 0.0, pltpu.roll(u[c], 127, axis=1))
        beside.append(near + far + up + down + right + left)
    conv = [None] * 10
    for n in range(5):
        for m in range(5):
            t = tile(5 * n + m)
            re, im = t * diff[n], t * diff[5 + n]
            conv[m] = re if n == 0 else conv[m] + re
            conv[5 + m] = im if n == 0 else conv[5 + m] + im
    step, diss, omega = step_ref[at, :], diss_ref[at, :], freq_ref[at, :]
    new = []
    for c in range(10):
        spin = omega * u[c + 5] if c < 5 else -(omega * u[c - 5])
        resid = conv[c] + spin + diss * (6.0 * u[c] - beside[c]) - source_ref[c, at, :]
        new.append(u[c] - step * resid)
    return new


def parts(value):
    high = value.astype(BF16).astype(F32)
    rest = value - high
    middle = rest.astype(BF16).astype(F32)
    return [high, middle, rest - middle]


def chosen(values, within):
    out = values[0]
    for k in range(1, 6):
        out = jnp.where(within == k, values[k], out)
    return out


def wall_terms(u_ref, fields_ref, walls, own_routing, beside):
    width = u_ref.shape[1]
    shape = (width, 128)
    lane, row = lanes(shape), rows(shape)
    within = lane % 8
    zero = jnp.zeros(shape, F32)
    at_wall = [zero + u_ref[c, :, 0:1] for c in range(10)]
    u = chosen([at_wall[c] for c in WALL], within)
    other = chosen([at_wall[(c + 5) % 10] for c in WALL], within)
    right = chosen([u_ref[c, :, 1:2] for c in WALL], within)
    down = jnp.where(row == 0, 0.0, pltpu.roll(u, 1, axis=0))
    up = jnp.where(row == width - 1, 0.0, pltpu.roll(u, width - 1, axis=0))
    own = u - fields_ref[0] * (
        fields_ref[2] * other + fields_ref[1] * (6.0 * u - (down + up + right)) - fields_ref[3]
    )

    def sent(route, weight, value):
        value = jnp.concatenate(parts(weight * jnp.where(within == 6, 1.0, value)), axis=1).astype(BF16)
        total = jnp.dot(route.astype(BF16), value, preferred_element_type=F32)
        return total[:, 0:128] + total[:, 128:256] + total[:, 256:384]

    routed = sent(*own_routing, own)
    even = lax.axis_index("brick") % 2 == 0
    for at, share in enumerate((-0.5, 0.5)):
        route, weight, diss = beside[at]
        share = jnp.where(even, -share, share)
        tile = jnp.where(even, walls[1 - at], walls[at])
        re, im = zero, zero
        for n in range(5):
            entry = pltpu.roll(tile, 127 - 5 * n, axis=1)
            re = re + entry * at_wall[n]
            im = im + entry * at_wall[5 + n]
        conv = jnp.where(lane < 3, re, jnp.where(lane < 6, pltpu.roll(im, 3, axis=1), 0.0))
        for turn in (8, 16, 32, 64):
            conv = conv + pltpu.roll(conv, turn, axis=1)
        routed = routed + sent(route, weight, diss * u + share * conv)
    return routed


def first_kernel(
    phase, recv_ref, u_ref, near_ref, far_ref, rim_ref, source_ref, step_ref, diss_ref, freq_ref,
    fields_ref, weight_ref, route_ref, out_ref, tiles_ref, rim_out_ref, code_ref, sum_ref, wide,
):
    rims = rims_beside(rim_ref, lax.axis_index("passage"), phase)
    width = u_ref.shape[1]
    for j in range(width):
        for m in range(QUADS):
            at = j * PITCH + 4 * m
            wide[at : at + 4, :] = recv_ref[j, :, 128 * m : 128 * m + 128].astype(F32)
    for e in range(25):
        tiles_ref[e] = wide[pl.ds(e, width, stride=PITCH), :].astype(BF16)
    rim_out_ref[...] = jnp.zeros_like(rim_out_ref)
    blocks = width // BLOCK
    scales = code_scale(near_ref, width), code_scale(far_ref, width)
    for b in range(blocks):
        new = sweep_block(
            b, blocks, u_ref, near_ref, far_ref, scales, rims,
            lambda e: wide[pl.ds(BLOCK * b * PITCH + e, BLOCK, stride=PITCH), :],
            source_ref, step_ref, diss_ref, freq_ref,
        )
        for c in range(10):
            out_ref[c, BLOCK * b : BLOCK * b + BLOCK, :] = new[c]
            if b == 0:
                rim_out_ref[0, c : c + 1, :] = new[c][0:1]
            if b == blocks - 1:
                rim_out_ref[1, c : c + 1, :] = new[c][BLOCK - 1 : BLOCK]
    coded(out_ref, code_ref)
    walls = [wide[pl.ds(25 + at, width, stride=PITCH), :] for at in range(2)]
    beside = [routing_beside(ref, width, CAP * (at + 1)) for at, ref in enumerate((near_ref, far_ref))]
    sum_ref[...] = wall_terms(out_ref, fields_ref, walls, (route_ref[...], weight_ref[...]), beside)


def second_kernel(
    phase, tiles_ref, u_ref, near_ref, far_ref, rim_ref, source_ref, step_ref, diss_ref, freq_ref, out_ref, after_ref
):
    rims = rims_beside(rim_ref, lax.axis_index("passage"), phase)
    width = u_ref.shape[1]
    blocks = width // BLOCK
    scales = code_scale(near_ref, width), code_scale(far_ref, width)
    for b in range(blocks):
        new = sweep_block(
            b, blocks, u_ref, near_ref, far_ref, scales, rims,
            lambda e: tiles_ref[e, BLOCK * b : BLOCK * b + BLOCK, :].astype(F32),
            source_ref, step_ref, diss_ref, freq_ref,
        )
        for c in range(10):
            out_ref[c, BLOCK * b : BLOCK * b + BLOCK, :] = new[c]
    after_ref[...] = jnp.zeros_like(after_ref)


def rim_kernel(phase, sum_ref, rim_ref, fields_ref, weight_ref, route_ref, send_ref):
    width = sum_ref.shape[0]
    within = lanes((1, 128)) % 8
    routed = sum_ref[...]
    for face, layer in zip((0, width - 1), rims_beside(rim_ref, lax.axis_index("passage"), phase)):
        value = chosen([jnp.zeros((1, 128), F32) + layer[c][:, 0:1] for c in WALL], within)
        at = slice(face, face + 1)
        value = weight_ref[at, :] * jnp.where(within == 6, 0.0, fields_ref[0, at, :] * fields_ref[1, at, :] * value)
        routed = routed + route_ref[:, at] * value
    for q in range(send_ref.shape[0]):
        send_ref[q] = routed[q : q + 1, :]


def nodes_kernel(recv_ref, after_ref, out_ref, dense):
    peers = recv_ref.shape[0]
    for q in range(peers):
        dense[q : q + 1, :] = recv_ref[q]
    node = lanes((peers, NODE_DEV)).astype(F32) + 1.0
    terms = parts(dense[...].T)
    total = jnp.zeros((24, NODE_DEV), F32)
    for first in range(0, CAP * PLANES, CAP):
        hits, values = [], []
        for r in range(first, first + CAP):
            hits.append(jnp.where(dense[:, 8 * r + 6 : 8 * r + 7] == node, 1.0, 0.0))
            values.append(jnp.concatenate([t[8 * r : 8 * r + 8, :] for t in terms], axis=0))
        hits, values = jnp.concatenate(hits, axis=0).astype(BF16), jnp.concatenate(values, axis=1).astype(BF16)
        total = total + jnp.dot(values, hits, preferred_element_type=F32)
    total = total[0:8] + total[8:16] + total[16:24]
    for c in range(6):
        out_ref[c] = total[c : c + 1, :]


def kernel_call(body, out, scratch=(), flops=None):
    whole = pl.BlockSpec(memory_space=pltpu.VMEM)
    return pl.pallas_call(
        body,
        out_shape=[jax.ShapeDtypeStruct(s, d) for s, d in out],
        out_specs=[whole] * len(out),
        scratch_shapes=list(scratch),
        compiler_params=pltpu.CompilerParams(vmem_limit_bytes=VMEM_BYTES),
        cost_estimate=flops and pl.CostEstimate(flops=flops, bytes_accessed=0, transcendentals=0),
    )


def planes_beside(code, bricks):
    near = [(i, i ^ 1) for i in range(bricks)]
    far = [(i, i - 1 if i % 2 == 0 else i + 1) for i in range(1, bricks - 1)]
    return lax.ppermute(code, "brick", near), lax.ppermute(code, "brick", far)


def swapped(rim, passes):
    return lax.ppermute(rim, "passage", [(i, (i + 1) % passes) for i in range(passes)])


def body(
    jac_blocks,
    psi_start,
    source,
    pseudo_step,
    dissipation,
    freq_volume,
    normals,
    face_owner,
    face_slot,
):
    passes = lax.axis_size("passage")
    bricks = lax.axis_size("brick")
    width, depth = psi_start.shape[3], psi_start.shape[4]
    phase = 2.0 * math.pi * ND * passes / BLADES
    field = (10, width, depth)
    rim = (2, 16, depth)
    plane = (10 * width + 16, depth)

    psi = psi_start.reshape(field)
    jac = jac_blocks.reshape(25, bricks, depth)
    source = source.reshape(field)
    scalars = [a.reshape(width, depth) for a in (pseudo_step, dissipation, freq_volume)]

    (send,) = kernel_call(
        prep_kernel,
        [((bricks, 4, QUADS * depth), BF16)],
        [pltpu.VMEM((ROWS * (bricks + 1), depth), F32)],
    )(jac)
    recv = lax.all_to_all(send, "brick", 0, 0, tiled=True)
    face = (width, 128)
    rims, weight, route, code, fields = kernel_call(
        aux_kernel,
        [(rim, F32), (face, F32), ((bricks, width), F32), ((plane[0] + 16, depth), I16), ((4, *face), F32)],
    )(psi, source, *scalars, face_owner.reshape(1, width), face_slot, normals.reshape(3, 1, width))
    rims = swapped(rims, passes)
    near, far = planes_beside(code, bricks)
    state, tiles, rims, code, terms = kernel_call(
        functools.partial(first_kernel, phase),
        [(field, F32), ((25, width, depth), BF16), (rim, F32), (plane, I16), (face, F32)],
        [pltpu.VMEM((PITCH * width, depth), F32)],
    )(recv, psi, near, far, rims, source, *scalars, fields, weight, route)

    rims = swapped(rims, passes)
    (routed,) = kernel_call(functools.partial(rim_kernel, phase), [((bricks, 1, 128), F32)], flops=AHEAD)(
        terms, rims, fields, weight, route
    )
    arrived = lax.all_to_all(routed, "brick", 0, 0, tiled=True)
    near, far = planes_beside(code, bricks)
    state, after = kernel_call(functools.partial(second_kernel, phase), [(field, F32), ((8, 128), F32)])(
        tiles, state, near, far, rims, source, *scalars
    )
    (sensitivity,) = kernel_call(nodes_kernel, [((6, 1, NODE_DEV), F32)], [pltpu.VMEM((bricks, 128), F32)])(
        arrived, after
    )
    return state.reshape(psi_start.shape), sensitivity.transpose(1, 0, 2)


def solution(mesh):
    placed = (
        P("passage", None, None, "brick"),
        P("passage", None, "brick", None, None),
        P("passage", None, "brick", None, None),
        P("passage", "brick", None, None),
        P("passage", "brick", None, None),
        P("passage", "brick", None, None),
        P("passage", None, "brick", None),
        P("passage", "brick", None),
        P("passage", "brick"),
    )
    return jax.shard_map(
        body,
        mesh=mesh,
        in_specs=placed,
        out_specs=(P("passage", None, "brick", None, None), P("passage", None, "brick")),
        check_vma=False,
    )
```

```python
import functools
import math

import jax
import jax.numpy as jnp
from jax import lax
from jax.experimental import pallas as pl
from jax.experimental.pallas import tpu as pltpu
from jax.sharding import PartitionSpec as P

NODE_DEV = 256
CAP = 4
PLANES = 3
WALL = (1, 2, 3, 6, 7, 8)
ND = 1
BLADES = 36
ROWS = 32
QUADS = 7
PITCH = ROWS + 1
BLOCK = 16
FULL = 32000.0
AHEAD = 1 << 34
VMEM_BYTES = 40 * 1024 * 1024
F32 = jnp.float32
BF16 = jnp.bfloat16
I16 = jnp.int16


def lanes(shape):
    return lax.broadcasted_iota(jnp.int32, shape, len(shape) - 1)


def rows(shape):
    return lax.broadcasted_iota(jnp.int32, shape, len(shape) - 2)


def prep_kernel(jac_ref, send_ref, wide):
    planes = jac_ref.shape[1]
    pitch = planes + 1
    wide[25 * pitch : ROWS * pitch, :] = jnp.zeros(((ROWS - 25) * pitch, 128), F32)
    lane = lanes((planes, 128))
    wall = jnp.zeros((planes, 128), F32)
    for e in range(25):
        entry = jac_ref[e].astype(F32)
        wide[e * pitch : e * pitch + planes, :] = entry
        wall = jnp.where(lane == e, pltpu.roll(entry, e, axis=1) if e else entry, wall)
    wide[25 * pitch + 1 : 25 * pitch + planes, :] = wall[0 : planes - 1]
    wide[26 * pitch : 26 * pitch + planes - 1, :] = wall[1:planes]
    for i in range(planes):
        plane = wide[pl.ds(i, ROWS, stride=pitch), :].astype(BF16)
        for m in range(QUADS):
            send_ref[i, :, 128 * m : 128 * m + 128] = plane[4 * m : 4 * m + 4]


def routing(owner_row, rank, values, first):
    faces = rank.shape[0]
    square = (faces, faces)
    lane = lanes((faces, 128))
    within = lane % 8
    weight = jnp.where(within == 6, values[3], 0.0)
    for d in range(3):
        weight = jnp.where((within == d) | (within == d + 3), values[d], weight)
    weight = jnp.where((lane // 8 - first).astype(F32) == rank, weight, 0.0)
    return jnp.where(rows(square).astype(F32) == owner_row, 1.0, 0.0), weight


def turned(value):
    length = max(value.shape)
    square = (length, length)
    eye = rows(square) == lanes(square)
    return jnp.sum(jnp.where(eye, value, 0.0), axis=1 if value.shape[0] == 1 else 0, keepdims=True)


def aux_kernel(
    psi_ref, source_ref, step_ref, diss_ref, freq_ref, owner_ref, slot_ref, normals_ref,
    rim_ref, weight_ref, route_ref, code_ref, fields_ref,
):
    width = psi_ref.shape[1]
    rim_ref[...] = jnp.zeros_like(rim_ref)
    for c in range(10):
        rim_ref[0, c : c + 1, :] = psi_ref[c, 0:1, :]
        rim_ref[1, c : c + 1, :] = psi_ref[c, width - 1 : width, :]

    square = (width, width)
    owner_row = owner_ref[...].astype(F32)
    owner = turned(owner_row)
    slot = turned(slot_ref[...].astype(F32)) + 1.0
    earlier = (owner == owner_row) & (lanes(square) < rows(square))
    rank = jnp.sum(jnp.where(earlier, 1.0, 0.0), axis=1, keepdims=True)
    normals = [turned(normals_ref[d]) for d in range(3)]
    route_ref[...], weight_ref[...] = routing(owner_row, rank, normals + [slot], 0)

    step, diss, omega = step_ref[:, 0:1], diss_ref[:, 0:1], freq_ref[:, 0:1]
    lane = lanes((width, 128))
    info = jnp.zeros((width, 128), F32)
    for k, value in enumerate([step * n for n in normals] + [slot, diss, owner, rank]):
        info = jnp.where(lane == k, value, info)
    coded(psi_ref, code_ref, info)

    within = lane % 8
    flow = jnp.zeros((width, 128), F32)
    for k, c in enumerate(WALL):
        flow = jnp.where(within == k, source_ref[c, :, 0:1], flow)
    fields_ref[0] = jnp.zeros((width, 128), F32) + step
    fields_ref[1] = jnp.zeros((width, 128), F32) + diss
    fields_ref[2] = jnp.where(within < 3, omega, -omega)
    fields_ref[3] = flow


def routing_beside(ref, width, first):
    last = 10 * width + 16
    exponent = ref[last - 16 : last, :].astype(jnp.int32).astype(F32)[15:16, :]
    packed = ref[last:, :].astype(jnp.int32).astype(F32)[0:8]
    code = [pltpu.roll(packed, 128 - 16 * g, axis=1) if g else packed for g in range(width // 8)]
    code = jnp.concatenate(code, axis=0)
    low = pltpu.roll(code, 120, axis=1)
    info = (code + low * (1.0 / FULL)) * (jnp.exp2(exponent) * (1.0 / FULL))
    column = [info[:, k : k + 1] for k in range(7)]
    slot, owner, rank = [jnp.round(column[k]) for k in (3, 5, 6)]
    return *routing(turned(owner), rank, column[:3] + [slot], first), column[4]


def exponent_of(top):
    return jnp.ceil(jnp.log2(jnp.maximum(top, 1e-30)))


def short(value):
    return jnp.round(value).astype(jnp.int32).astype(I16)


def coded(u_ref, code_ref, info=None):
    width = u_ref.shape[1]
    exponents = jnp.zeros((16, 128), F32)
    row = rows((16, 128))
    for c in range(10):
        top = jnp.max(jnp.abs(u_ref[c]), axis=0, keepdims=True)
        top = jnp.max(top, axis=1, keepdims=True)
        exponent = exponent_of(top)
        code_ref[c * width : (c + 1) * width, :] = short(u_ref[c] * (FULL * jnp.exp2(-exponent)))
        exponents = jnp.where(row == c, exponent, exponents)
    if info is not None:
        exponent = exponent_of(jnp.max(jnp.abs(info), axis=0, keepdims=True))
        exponents = jnp.where(row == 15, exponent, exponents)
        value = info * (FULL * jnp.exp2(-exponent))
        high = jnp.round(value)
        low = jnp.round((value - high) * FULL)
        lane = lanes((width, 128))
        both = jnp.where(lane < 8, high, jnp.where(lane < 16, pltpu.roll(low, 8, axis=1), 0.0))
        packed = both[0:8]
        for g in range(1, width // 8):
            packed = packed + pltpu.roll(both[8 * g : 8 * g + 8], 16 * g, axis=1)
        code_ref[10 * width + 16 :, :] = short(jnp.concatenate([packed, jnp.zeros((8, 128), F32)], axis=0))
    code_ref[10 * width : 10 * width + 16, :] = short(exponents)


def code_scale(code_ref, width):
    exponents = code_ref[10 * width : 10 * width + 16, :].astype(jnp.int32).astype(F32)
    scale = jnp.exp2(exponents) * (1.0 / FULL)
    return [scale[c : c + 1, :] for c in range(10)]


def rims_beside(rim_ref, passage, phase):
    def rotated(at, turn, edge):
        cosine = jnp.where(passage == edge, math.cos(turn), 1.0)
        sine = jnp.where(passage == edge, math.sin(turn), 0.0)
        rim = [rim_ref[at, c : c + 1, :] for c in range(10)]
        re = [rim[n] * cosine - rim[5 + n] * sine for n in range(5)]
        im = [rim[n] * sine + rim[5 + n] * cosine for n in range(5)]
        return re + im

    return rotated(1, -phase, 0), rotated(0, phase, 1)


def sweep_block(b, blocks, u_ref, near_ref, far_ref, scales, rims, tile, source_ref, step_ref, diss_ref, freq_ref):
    at = slice(BLOCK * b, BLOCK * b + BLOCK)
    shape = (BLOCK, 128)
    row, lane = rows(shape), lanes(shape)
    width = u_ref.shape[1]
    u = [u_ref[c, at, :] for c in range(10)]

    if b == 0:
        before = rims[0]
    else:
        before = [u_ref[c, BLOCK * b - 1 : BLOCK * b, :] for c in range(10)]
    if b == blocks - 1:
        after = rims[1]
    else:
        after = [u_ref[c, BLOCK * b + BLOCK : BLOCK * b + BLOCK + 1, :] for c in range(10)]

    half = jnp.where(lax.axis_index("brick") % 2 == 0, 0.5, -0.5)
    diff = []
    beside = []
    for c in range(10):
        first = c * width + BLOCK * b
        near = near_ref[first : first + BLOCK, :].astype(jnp.int32).astype(F32) * scales[0][c]
        far = far_ref[first : first + BLOCK, :].astype(jnp.int32).astype(F32) * scales[1][c]
        diff.append(half * (near - far))
        down = jnp.where(row == 0, before[c], pltpu.roll(u[c], 1, axis=0))
        up = jnp.where(row == BLOCK - 1, after[c], pltpu.roll(u[c], BLOCK - 1, axis=0))
        left = jnp.where(lane == 0, 0.0, pltpu.roll(u[c], 1, axis=1))
        right = jnp.where(lane == 127, 0.0, pltpu.roll(u[c], 127, axis=1))
        beside.append(near + far + up + down + right + left)
    conv = [None] * 10
    for n in range(5):
        for m in range(5):
            t = tile(5 * n + m)
            re, im = t * diff[n], t * diff[5 + n]
            conv[m] = re if n == 0 else conv[m] + re
            conv[5 + m] = im if n == 0 else conv[5 + m] + im
    step, diss, omega = step_ref[at, :], diss_ref[at, :], freq_ref[at, :]
    new = []
    for c in range(10):
        spin = omega * u[c + 5] if c < 5 else -(omega * u[c - 5])
        resid = conv[c] + spin + diss * (6.0 * u[c] - beside[c]) - source_ref[c, at, :]
        new.append(u[c] - step * resid)
    return new


def parts(value):
    high = value.astype(BF16).astype(F32)
    rest = value - high
    middle = rest.astype(BF16).astype(F32)
    return [high, middle, rest - middle]


def chosen(values, within):
    out = values[0]
    for k in range(1, 6):
        out = jnp.where(within == k, values[k], out)
    return out


def wall_terms(u_ref, fields_ref, walls, own_routing, beside):
    width = u_ref.shape[1]
    shape = (width, 128)
    lane, row = lanes(shape), rows(shape)
    within = lane % 8
    zero = jnp.zeros(shape, F32)
    at_wall = [zero + u_ref[c, :, 0:1] for c in range(10)]
    u = chosen([at_wall[c] for c in WALL], within)
    other = chosen([at_wall[(c + 5) % 10] for c in WALL], within)
    right = chosen([u_ref[c, :, 1:2] for c in WALL], within)
    down = jnp.where(row == 0, 0.0, pltpu.roll(u, 1, axis=0))
    up = jnp.where(row == width - 1, 0.0, pltpu.roll(u, width - 1, axis=0))
    own = u - fields_ref[0] * (
        fields_ref[2] * other + fields_ref[1] * (6.0 * u - (down + up + right)) - fields_ref[3]
    )

    def sent(route, weight, value):
        value = jnp.concatenate(parts(weight * jnp.where(within == 6, 1.0, value)), axis=1).astype(BF16)
        total = jnp.dot(route.astype(BF16), value, preferred_element_type=F32)
        return total[:, 0:128] + total[:, 128:256] + total[:, 256:384]

    routed = sent(*own_routing, own)
    even = lax.axis_index("brick") % 2 == 0
    for at, share in enumerate((-0.5, 0.5)):
        route, weight, diss = beside[at]
        share = jnp.where(even, -share, share)
        tile = jnp.where(even, walls[1 - at], walls[at])
        re, im = zero, zero
        for n in range(5):
            entry = pltpu.roll(tile, 127 - 5 * n, axis=1)
            re = re + entry * at_wall[n]
            im = im + entry * at_wall[5 + n]
        conv = jnp.where(lane < 3, re, jnp.where(lane < 6, pltpu.roll(im, 3, axis=1), 0.0))
        for turn in (8, 16, 32, 64):
            conv = conv + pltpu.roll(conv, turn, axis=1)
        routed = routed + sent(route, weight, diss * u + share * conv)
    return routed


def widened(recv_ref, wide, width):
    for j in range(width):
        for m in range(QUADS):
            at = j * PITCH + 4 * m
            wide[at : at + 4, :] = recv_ref[j, :, 128 * m : 128 * m + 128].astype(F32)


def first_kernel(
    phase, recv_ref, u_ref, near_ref, far_ref, rim_ref, source_ref, step_ref, diss_ref, freq_ref,
    fields_ref, weight_ref, route_ref, out_ref, rim_out_ref, code_ref, sum_ref, wide,
):
    rims = rims_beside(rim_ref, lax.axis_index("passage"), phase)
    width = u_ref.shape[1]
    widened(recv_ref, wide, width)
    rim_out_ref[...] = jnp.zeros_like(rim_out_ref)
    blocks = width // BLOCK
    scales = code_scale(near_ref, width), code_scale(far_ref, width)
    for b in range(blocks):
        new = sweep_block(
            b, blocks, u_ref, near_ref, far_ref, scales, rims,
            lambda e: wide[pl.ds(BLOCK * b * PITCH + e, BLOCK, stride=PITCH), :],
            source_ref, step_ref, diss_ref, freq_ref,
        )
        for c in range(10):
            out_ref[c, BLOCK * b : BLOCK * b + BLOCK, :] = new[c]
            if b == 0:
                rim_out_ref[0, c : c + 1, :] = new[c][0:1]
            if b == blocks - 1:
                rim_out_ref[1, c : c + 1, :] = new[c][BLOCK - 1 : BLOCK]
    coded(out_ref, code_ref)
    walls = [wide[pl.ds(25 + at, width, stride=PITCH), :] for at in range(2)]
    beside = [routing_beside(ref, width, CAP * (at + 1)) for at, ref in enumerate((near_ref, far_ref))]
    sum_ref[...] = wall_terms(out_ref, fields_ref, walls, (route_ref[...], weight_ref[...]), beside)


def second_kernel(
    phase, recv_ref, u_ref, near_ref, far_ref, rim_ref, source_ref, step_ref, diss_ref, freq_ref, out_ref, after_ref,
    wide,
):
    rims = rims_beside(rim_ref, lax.axis_index("passage"), phase)
    width = u_ref.shape[1]
    widened(recv_ref, wide, width)
    blocks = width // BLOCK
    scales = code_scale(near_ref, width), code_scale(far_ref, width)
    for b in range(blocks):
        new = sweep_block(
            b, blocks, u_ref, near_ref, far_ref, scales, rims,
            lambda e: wide[pl.ds(BLOCK * b * PITCH + e, BLOCK, stride=PITCH), :],
            source_ref, step_ref, diss_ref, freq_ref,
        )
        for c in range(10):
            out_ref[c, BLOCK * b : BLOCK * b + BLOCK, :] = new[c]
    after_ref[...] = jnp.zeros_like(after_ref)


def rim_kernel(phase, sum_ref, rim_ref, fields_ref, weight_ref, route_ref, send_ref):
    width = sum_ref.shape[0]
    within = lanes((1, 128)) % 8
    routed = sum_ref[...]
    for face, layer in zip((0, width - 1), rims_beside(rim_ref, lax.axis_index("passage"), phase)):
        value = chosen([jnp.zeros((1, 128), F32) + layer[c][:, 0:1] for c in WALL], within)
        at = slice(face, face + 1)
        value = weight_ref[at, :] * jnp.where(within == 6, 0.0, fields_ref[0, at, :] * fields_ref[1, at, :] * value)
        routed = routed + route_ref[:, at] * value
    for q in range(send_ref.shape[0]):
        send_ref[q] = routed[q : q + 1, :]


def nodes_kernel(recv_ref, after_ref, out_ref, dense):
    peers = recv_ref.shape[0]
    for q in range(peers):
        dense[q : q + 1, :] = recv_ref[q]
    node = lanes((peers, NODE_DEV)).astype(F32) + 1.0
    terms = parts(dense[...].T)
    total = jnp.zeros((24, NODE_DEV), F32)
    for first in range(0, CAP * PLANES, CAP):
        hits, values = [], []
        for r in range(first, first + CAP):
            hits.append(jnp.where(dense[:, 8 * r + 6 : 8 * r + 7] == node, 1.0, 0.0))
            values.append(jnp.concatenate([t[8 * r : 8 * r + 8, :] for t in terms], axis=0))
        hits, values = jnp.concatenate(hits, axis=0).astype(BF16), jnp.concatenate(values, axis=1).astype(BF16)
        total = total + jnp.dot(values, hits, preferred_element_type=F32)
    total = total[0:8] + total[8:16] + total[16:24]
    for c in range(6):
        out_ref[c] = total[c : c + 1, :]


def kernel_call(body, out, scratch=(), flops=None):
    whole = pl.BlockSpec(memory_space=pltpu.VMEM)
    return pl.pallas_call(
        body,
        out_shape=[jax.ShapeDtypeStruct(s, d) for s, d in out],
        out_specs=[whole] * len(out),
        scratch_shapes=list(scratch),
        compiler_params=pltpu.CompilerParams(vmem_limit_bytes=VMEM_BYTES),
        cost_estimate=flops and pl.CostEstimate(flops=flops, bytes_accessed=0, transcendentals=0),
    )


def planes_beside(code, bricks):
    near = [(i, i ^ 1) for i in range(bricks)]
    far = [(i, i - 1 if i % 2 == 0 else i + 1) for i in range(1, bricks - 1)]
    return lax.ppermute(code, "brick", near), lax.ppermute(code, "brick", far)


def swapped(rim, passes):
    return lax.ppermute(rim, "passage", [(i, (i + 1) % passes) for i in range(passes)])


def body(
    jac_blocks,
    psi_start,
    source,
    pseudo_step,
    dissipation,
    freq_volume,
    normals,
    face_owner,
    face_slot,
):
    passes = lax.axis_size("passage")
    bricks = lax.axis_size("brick")
    width, depth = psi_start.shape[3], psi_start.shape[4]
    phase = 2.0 * math.pi * ND * passes / BLADES
    field = (10, width, depth)
    rim = (2, 16, depth)
    plane = (10 * width + 16, depth)

    psi = psi_start.reshape(field)
    jac = jac_blocks.reshape(25, bricks, depth)
    source = source.reshape(field)
    scalars = [a.reshape(width, depth) for a in (pseudo_step, dissipation, freq_volume)]

    (send,) = kernel_call(
        prep_kernel,
        [((bricks, 4, QUADS * depth), BF16)],
        [pltpu.VMEM((ROWS * (bricks + 1), depth), F32)],
    )(jac)
    recv = lax.all_to_all(send, "brick", 0, 0, tiled=True)
    face = (width, 128)
    rims, weight, route, code, fields = kernel_call(
        aux_kernel,
        [(rim, F32), (face, F32), ((bricks, width), F32), ((plane[0] + 16, depth), I16), ((4, *face), F32)],
    )(psi, source, *scalars, face_owner.reshape(1, width), face_slot, normals.reshape(3, 1, width))
    rims = swapped(rims, passes)
    near, far = planes_beside(code, bricks)
    state, rims, code, terms = kernel_call(
        functools.partial(first_kernel, phase),
        [(field, F32), (rim, F32), (plane, I16), (face, F32)],
        [pltpu.VMEM((PITCH * width, depth), F32)],
    )(recv, psi, near, far, rims, source, *scalars, fields, weight, route)

    rims = swapped(rims, passes)
    (routed,) = kernel_call(functools.partial(rim_kernel, phase), [((bricks, 1, 128), F32)], flops=AHEAD)(
        terms, rims, fields, weight, route
    )
    arrived = lax.all_to_all(routed, "brick", 0, 0, tiled=True)
    near, far = planes_beside(code, bricks)
    state, after = kernel_call(
        functools.partial(second_kernel, phase),
        [(field, F32), ((8, 128), F32)],
        [pltpu.VMEM((PITCH * width, depth), F32)],
    )(
        recv, state, near, far, rims, source, *scalars
    )
    (sensitivity,) = kernel_call(nodes_kernel, [((6, 1, NODE_DEV), F32)], [pltpu.VMEM((bricks, 128), F32)])(
        arrived, after
    )
    return state.reshape(psi_start.shape), sensitivity.transpose(1, 0, 2)


def solution(mesh):
    placed = (
        P("passage", None, None, "brick"),
        P("passage", None, "brick", None, None),
        P("passage", None, "brick", None, None),
        P("passage", "brick", None, None),
        P("passage", "brick", None, None),
        P("passage", "brick", None, None),
        P("passage", None, "brick", None),
        P("passage", "brick", None),
        P("passage", "brick"),
    )
    return jax.shard_map(
        body,
        mesh=mesh,
        in_specs=placed,
        out_specs=(P("passage", None, "brick", None, None), P("passage", None, "brick")),
        check_vma=False,
    )
```
